512 devices in a mesh: dp: 4 (over x_lo, core), ctx: 128 (over z, x_hi, y).
Axes of the slice: x: 4 (x_hi: 2, x_lo: 2; x = x_hi * 2 + x_lo), y: 4, z: 16, core: 2. Of those that a mesh axis runs over, the one named last changes fastest.
Arguments:
- features: bfloat16 [4, 16384, 4096], P('dp', 'ctx'), may hold values from -6 to 6
- gate_values: bfloat16 [4, 16384, 4096], P('dp', 'ctx'), may hold values from -6 to 6
- upstream: bfloat16 [4, 16384, 4096], P('dp', 'ctx'), may hold values from -6 to 6
- short_filter: float32 [7, 4096], replicated, may hold values from -2 to 2
- long_filter: bfloat16 [32, 4096], replicated, may hold values from -0.09375 to 0.09375
- loss_scale: float32 [1], replicated, may hold values from 8 to 64
Outputs:
- input_grad: bfloat16 [4, 16384, 4096], P('dp', 'ctx')
- short_grad: float32 [7, 4096], P(None, 'ctx')
- grad_norm: float32 [1], replicated
The draws below stay inside these ranges and needn't reach their ends.
All inputs are finite; a program needn't handle non-finite values.
Results may differ from the reference program's by a relative error of at most 0.0057.
Values may be sent and summed in bfloat16 or wider, within the bound.
No kernel may reach another device: no remote copies, remote signals or barrier semaphores. Data moves between devices by JAX's collectives and lax.ppermute only.
A program may use at most 128 MiB of HBM per device.

```python
import math
import jax
import jax.numpy as jnp
from jax import lax

C = 4096
TAPS = 4096
G = 32
BATCH = 4
LEN = 16384


def level_of(rng, dims, cuts, low, high):
    loudness, own = 1.0, jax.random.fold_in(rng, 6)
    for dim, parts in cuts:
        draws = jnp.exp(jax.random.uniform(jax.random.fold_in(own, dim), (parts,), jnp.float32, low / len(cuts), high / len(cuts)))
        loudness = loudness * jnp.repeat(draws, dims[dim] // parts).reshape([-1 if axis == dim else 1 for axis in range(len(dims))])
    return loudness


def noise(stream_key, dims, spread, reach, shards=(), dtype=jnp.bfloat16):
    loudness = level_of(stream_key, dims, shards, -0.22, 0.18) if shards else 1.0
    array = jax.random.normal(stream_key, dims, jnp.float32) * spread * loudness
    return jnp.minimum(jnp.maximum(array, -reach), reach).astype(dtype)


def setup_inputs(seed: int = 0) -> dict:
    key_of = jax.random.split(jax.random.key(seed), 7)
    features = noise(key_of[0], (BATCH, LEN, C), 1.0, 6.0, ((0, 4), (1, 128)))
    gate_values = noise(key_of[1], (BATCH, LEN, C), 1.0, 6.0, ((0, 4), (1, 128)))
    upstream = noise(key_of[2], (BATCH, LEN, C), 1.0, 6.0, ((0, 4), (1, 128)))
    short_filter = noise(key_of[3], (7, C), 7 ** -0.5, 2.0, (), jnp.float32)
    long_filter = noise(key_of[4], (G, TAPS), TAPS ** -0.5, 0.09375)
    loss_scale = jnp.clip(jnp.exp(jax.random.uniform(key_of[5], (1,), jnp.float32, math.log(8.0), math.log(64.0))), 8.0, 64.0)
    return {"features": features, "gate_values": gate_values, "upstream": upstream, "short_filter": short_filter, "long_filter": long_filter, "loss_scale": loss_scale}


def reference(features, gate_values, upstream, short_filter, long_filter, loss_scale):
    gated = (upstream.astype(jnp.float32) * gate_values.astype(jnp.float32)).astype(jnp.bfloat16)
    member = jnp.arange(C) // (C // G)
    chan_taps = long_filter.astype(jnp.float32)[member]
    length_fft = 2 ** math.ceil(math.log2(LEN + TAPS))
    spectrum = jnp.fft.rfft(chan_taps, n=length_fft, axis=1).T

    def one_sequence(sequence):
        values = jnp.fft.rfft(sequence.astype(jnp.float32), n=length_fft, axis=0)
        result = jnp.fft.irfft(values * jnp.conj(spectrum), n=length_fft, axis=0)
        return result[:LEN].astype(jnp.bfloat16)
    conv_grad = lax.map(one_sequence, gated)
    width = short_filter.shape[0]
    rim = width - 1
    conv_wide = conv_grad.astype(jnp.float32)
    extended = jnp.pad(conv_wide, ((0, 0), (0, rim), (0, 0)))
    input_grad = jnp.zeros(conv_wide.shape, jnp.float32)
    for position in range(width):
        input_grad = input_grad + short_filter[position] * extended[:, position:position + LEN]
    earlier = jnp.pad(features.astype(jnp.float32), ((0, 0), (rim, 0), (0, 0)))
    row_terms = []
    for position in range(width):
        shifted = earlier[:, rim - position:rim - position + LEN]
        row_terms.append(jnp.einsum('stc,stc->c', conv_wide, shifted))
    unscaled = jnp.stack(row_terms) / loss_scale[0]
    norm_value = jnp.sqrt(jnp.sum(unscaled * unscaled))
    short_grad = jnp.where(jnp.isfinite(norm_value), unscaled, jnp.zeros_like(unscaled))
    return (input_grad.astype(jnp.bfloat16), short_grad, norm_value.reshape(1))
```

```python
import functools

import jax
import jax.numpy as jnp
from jax import lax
from jax.experimental import pallas as pl
from jax.experimental.pallas import tpu as pltpu
from jax.sharding import PartitionSpec as P

PLANE = 8
BLK = 256
GW = 128
HEAD = 16
SHORT = 64
VMEM = 56 * 1024 * 1024
F32, BF16 = jnp.float32, jnp.bfloat16


def params(grid=True):
    kwargs = {"dimension_semantics": ("arbitrary",)} if grid else {}
    return pltpu.CompilerParams(vmem_limit_bytes=VMEM, **kwargs)


def cost(flops, nbytes):
    return pl.CostEstimate(
        flops=int(flops) // SHORT, bytes_accessed=int(nbytes) // SHORT, transcendentals=0
    )


def dot(a, b):
    return jnp.dot(a, b, preferred_element_type=F32)


def gate_kernel(up_ref, gate_ref, out_ref):
    width = out_ref.shape[2]
    for p in range(PLANE):
        cols = slice(p * width, (p + 1) * width)
        prod = up_ref[0, :, cols].astype(F32) * gate_ref[0, :, cols].astype(F32)
        out_ref[p] = prod.astype(BF16)


def gate(upstream, gates):
    _, rows, chans = upstream.shape
    return pl.pallas_call(
        gate_kernel,
        out_shape=jax.ShapeDtypeStruct((PLANE, rows, chans // PLANE), BF16),
        compiler_params=params(False),
        cost_estimate=cost(upstream.size, 6 * upstream.size),
        name="gate",
    )(upstream, gates)


def pack_kernel(src_ref, out_ref):
    width = out_ref.shape[2]
    for p in range(PLANE):
        out_ref[p] = src_ref[0, :, p * width : (p + 1) * width]


def pack(features):
    _, rows, chans = features.shape
    return pl.pallas_call(
        pack_kernel,
        out_shape=jax.ShapeDtypeStruct((PLANE, rows, chans // PLANE), BF16),
        compiler_params=params(False),
        cost_estimate=cost(0, 4 * features.size),
        name="pack",
    )(features)


def split_terms(x):
    high = x.astype(BF16)
    rest = x - high.astype(F32)
    mid = rest.astype(BF16)
    return high, mid, (rest - mid.astype(F32)).astype(BF16)


def prepare_kernel(lane, half_ref, scale_ref, copies, out_ref):
    total = copies[0]
    for n in range(1, copies.shape[0]):
        total = total + copies[n]
    unscaled = total / scale_ref[0]
    norm = jnp.sum(unscaled * unscaled, keepdims=True)
    norm = split_terms(jnp.broadcast_to(norm, (8, 8)))
    span = PLANE * lane
    mine = unscaled[:, :span]
    for n in range(1, unscaled.shape[1] // span):
        mine = jnp.where(half_ref[0] == n, unscaled[:, n * span : (n + 1) * span], mine)
    parts = split_terms(mine)
    pad = jnp.zeros((8, GW - 3 * lane - 24), BF16)
    for p in range(PLANE):
        row = [x[:, p * lane : (p + 1) * lane] for x in parts]
        tile = jnp.concatenate([*row, *norm, pad], axis=1).astype(F32)
        out_ref[p] = jnp.concatenate([tile, jnp.zeros_like(tile)], axis=0).astype(BF16)


def prepare(half, scale, copies, lane):
    return pl.pallas_call(
        functools.partial(prepare_kernel, lane),
        in_specs=[pl.BlockSpec(memory_space=pltpu.SMEM)] * 2 + [pl.BlockSpec(memory_space=pltpu.VMEM)],
        out_shape=jax.ShapeDtypeStruct((PLANE, HEAD, GW), BF16),
        compiler_params=params(False),
        cost_estimate=cost(copies.size, 4 * copies.size),
        name="prepare",
    )(half.reshape(1), scale, copies)


def unpack_kernel(lane, source_ref, got, out_ref, short_ref, norm_ref):
    width = got.shape[2]
    rows = out_ref.shape[1]
    norm = jnp.zeros((8, 1), F32)
    short = jnp.zeros((8, lane), F32)
    for p in range(PLANE):
        out_ref[0, :, p * width : (p + 1) * width] = got[p, :rows, :]
        tile = got[p, rows:, :GW].astype(F32)[:8]
        at = 3 * lane
        norm = norm + (tile[:, at : at + 1] + tile[:, at + 8 : at + 9] + tile[:, at + 16 : at + 17])
        terms = tile[:, :lane] + tile[:, lane : 2 * lane] + tile[:, 2 * lane : 3 * lane]
        short = jnp.where(source_ref[0] == p, terms, short)
    norm = jnp.sqrt(norm)
    short = jnp.where(jnp.abs(norm) < jnp.inf, short, jnp.zeros_like(short))
    short_ref[...] = short[: short_ref.shape[0], :]
    norm_ref[...] = norm[:1, :]


def unpack(source, got, rows, width, lane):
    return pl.pallas_call(
        functools.partial(unpack_kernel, lane),
        in_specs=[pl.BlockSpec(memory_space=pltpu.SMEM), pl.BlockSpec(memory_space=pltpu.VMEM)],
        out_shape=[
            jax.ShapeDtypeStruct((1, rows, PLANE * got.shape[2]), BF16),
            jax.ShapeDtypeStruct((width, lane), F32),
            jax.ShapeDtypeStruct((1, 1), F32),
        ],
        compiler_params=params(False),
        cost_estimate=cost(0, 4 * got.size),
        name="unpack",
    )(source.reshape(1), got)


def toeplitz_kernel(taps_ref, all_ref, far_ref):
    taps = taps_ref.shape[2]
    half = BLK // 2
    row = jnp.concatenate([taps_ref[0], jnp.zeros((1, BLK), F32)], axis=1)
    base = jnp.broadcast_to(row, (half, taps + BLK))
    base = pltpu.roll(base, 0, 1, stride=1, stride_axis=0).astype(BF16)
    all_ref[0, :half, :] = base
    all_ref[0, half:, :half] = jnp.zeros((half, half), BF16)
    all_ref[0, half:, half:] = base[:, : taps + BLK - half]
    far_ref[0] = all_ref[0, :, taps - 7 * BLK :]


def toeplitz(filters):
    groups, taps = filters.shape
    return pl.pallas_call(
        toeplitz_kernel,
        grid=(groups,),
        in_specs=[pl.BlockSpec((1, 1, taps), lambda g: (g, 0, 0))],
        out_specs=[
            pl.BlockSpec((1, BLK, taps + BLK), lambda g: (g, 0, 0)),
            pl.BlockSpec((1, BLK, 8 * BLK), lambda g: (g, 0, 0)),
        ],
        out_shape=[
            jax.ShapeDtypeStruct((groups, BLK, taps + BLK), BF16),
            jax.ShapeDtypeStruct((groups, BLK, 8 * BLK), BF16),
        ],
        compiler_params=params(),
        cost_estimate=cost(groups * BLK * taps * 16, 2 * groups * BLK * taps * 3),
        name="toeplitz",
    )(filters.astype(F32).reshape(groups, 1, taps))


def fill_pairs(pairs_ref, planes):
    rows = sum(x.shape[0] for x in planes)
    zero = jnp.zeros((BLK, GW), BF16)
    pairs_ref[:BLK, :GW] = zero
    at = 0
    for x in planes:
        pairs_ref[BLK + at : BLK + at + x.shape[0], :GW] = x[...]
        pairs_ref[at : at + x.shape[0], GW:] = x[...]
        at += x.shape[0]
    pairs_ref[rows : rows + BLK, GW:] = zero


def tile_products(tiles_ref, first, last, pairs_ref, distance, blocks):
    out = []
    for pair in (0, 2):
        low, high = distance - 1 - pair, distance + blocks - 1 - pair
        k0, k1 = max(low, first), min(high, last)
        tiles = tiles_ref[0, :, (k0 - first) * BLK : (k1 + 1 - first) * BLK]
        window = pairs_ref[(k0 - low) * BLK : (k1 + 1 - low) * BLK, :]
        out.append(dot(tiles, window))
    return out


def store_rows(ref, products, add=None):
    for n, prod in enumerate(products):
        for m in range(2):
            rows = slice((2 * n + m) * BLK, (2 * n + m + 1) * BLK)
            value = prod[:, m * GW : (m + 1) * GW]
            ref[rows, :] = value if add is None else add[rows, :] + value


def correlate(conv_ref, feat_ref, before, feat_wide, terms):
    rows = conv_ref.shape[0]
    feat_wide[:8, :] = before[before.shape[0] - 8 :, :].astype(F32)
    feat_wide[8:, :] = feat_ref[...].astype(F32)
    for r in range(0, rows, 128):
        conv = conv_ref[r : r + 128, :]
        for j in range(len(terms)):
            prod = conv * feat_wide[r + 8 - j : r + 136 - j, :]
            terms[j] = terms[j] + jnp.sum(prod.reshape(16, 8, GW), axis=0)
    return terms


def add_terms(raw_ref, terms, add=None):
    out = [jnp.sum(t, axis=0, keepdims=True) for t in terms]
    out.append(jnp.zeros((8 - len(terms), GW), F32))
    out = jnp.concatenate(out, axis=0)
    raw_ref[...] = out if add is None else add[...] + out


def put_terms(raw_ref, terms, add=None):
    out = [jnp.sum(t, axis=0, keepdims=True) for t in terms]
    out.append(jnp.zeros((8 - len(terms), GW), F32))
    out = jnp.concatenate(out, axis=0)
    raw_ref[...] = out if add is None else add[...] + out


def by_group(kernel, name, flops, args, outs, scratch):
    groups = outs[0].shape[1] // GW

    def spec(x):
        if len(x.shape) == 3:
            return pl.BlockSpec((1,) + x.shape[1:], lambda g: (g, 0, 0))
        return pl.BlockSpec((x.shape[0], GW), lambda g: (0, g))

    moved = sum(x.size * x.dtype.itemsize for x in (*args, *outs))
    return pl.pallas_call(
        kernel,
        grid=(groups,),
        in_specs=[spec(x) for x in args],
        out_specs=[spec(x) for x in outs],
        out_shape=outs,
        scratch_shapes=scratch,
        compiler_params=params(),
        cost_estimate=cost(flops * groups, moved),
        name=name,
    )(*args)


def pairs_of(rows):
    return pltpu.VMEM((rows + BLK, 2 * GW), BF16)


def early_kernel(x0, x1, tiles, acc_ref, mid_ref, pairs):
    last = tiles.shape[2] // BLK - 1
    fill_pairs(pairs, [x0, x1])
    store_rows(acc_ref, tile_products(tiles, 0, last, pairs, 0, 8))
    fill_pairs(pairs, [x1])
    store_rows(mid_ref, tile_products(tiles, 0, last, pairs, 8, 4))


def early(x0, x1, tiles):
    rows, own = x0.shape
    out = jax.ShapeDtypeStruct((rows, own), F32)
    return by_group(
        early_kernel, "early", 24 * rows * rows * GW, [x0, x1, tiles], [out, out], [pairs_of(2 * rows)]
    )


def own_terms_kernel(width, acc, f0, f1, raw_ref, feat_wide):
    terms = [jnp.zeros((8, GW), F32)] * width
    before = f1[f1.shape[0] - HEAD :, :]
    put_terms(raw_ref, correlate(acc, f0, before, feat_wide, terms))


def own_terms(width, acc, f0, f1):
    rows, own = acc.shape
    out = jax.ShapeDtypeStruct((8, own), F32)
    scratch = [pltpu.VMEM((rows + 8, GW), F32)]
    kernel = functools.partial(own_terms_kernel, width)
    return by_group(kernel, "own_terms", 14 * rows * GW, [acc, f0, f1], [out], scratch)[0]


def far_terms_kernel(width, mid, raw, x2, f1, f2, f3_tail, tiles, raw_ref, pairs, far, feat_wide):
    fill_pairs(pairs, [x2])
    terms = [jnp.zeros((8, GW), F32)] * width
    before = f2[f2.shape[0] - HEAD :, :]
    store_rows(far, tile_products(tiles, 9, 16, pairs, 12, 4), add=mid)
    terms = correlate(far, f1, before, feat_wide, terms)
    store_rows(far, tile_products(tiles, 9, 16, pairs, 16, 4))
    terms = correlate(far, f2, f3_tail[...], feat_wide, terms)
    put_terms(raw_ref, terms, add=raw)


def far_terms(width, mid, raw, x2, f1, f2, f3_tail, tiles):
    rows, own = mid.shape
    out = jax.ShapeDtypeStruct((8, own), F32)
    scratch = [pairs_of(rows), pltpu.VMEM((rows, GW), F32), pltpu.VMEM((rows + 8, GW), F32)]
    kernel = functools.partial(far_terms_kernel, width)
    args = [mid, raw, x2, f1, f2, f3_tail, tiles]
    return by_group(kernel, "far_terms", 16 * rows * rows * GW, args, [out], scratch)[0]


def third_kernel(acc_in, x2, x3, x4_head, tiles, acc_ref, head_ref, pairs):
    last = tiles.shape[2] // BLK - 1
    fill_pairs(pairs, [x2, x3])
    store_rows(acc_ref, tile_products(tiles, 0, last, pairs, 8, 8), add=acc_in)
    ahead = jnp.concatenate([x4_head[...], jnp.zeros((GW - HEAD, GW), BF16)], axis=0)
    corner = tiles[0, :HEAD, last * BLK : last * BLK + GW]
    head_ref[...] = (acc_ref[:HEAD, :] + dot(corner, ahead)).astype(BF16)


def third(acc, x2, x3, x4_head, tiles):
    rows, own = acc.shape
    outs = [jax.ShapeDtypeStruct((rows, own), F32), jax.ShapeDtypeStruct((HEAD, own), BF16)]
    args = [acc, x2, x3, x4_head, tiles]
    return by_group(third_kernel, "third", 18 * rows * rows * GW, args, outs, [pairs_of(2 * rows)])


def last_kernel(width, acc_in, x4, tiles, next_head, taps, extra, out_ref, pairs, wide):
    rows = x4.shape[0]
    step = rows // PLANE
    fill_pairs(pairs, [x4])
    for n, prod in enumerate(tile_products(tiles, 13, 16, pairs, 16, 4)):
        for m in range(2):
            at = slice((2 * n + m) * BLK, (2 * n + m + 1) * BLK)
            value = acc_in[at, :] + prod[:, m * GW : (m + 1) * GW]
            wide[at, :] = value.astype(BF16).astype(F32)
    wide[rows:, :] = next_head[:8, :].astype(F32)
    for r in range(PLANE):
        total = taps[0:1, :] * wide[r * step : (r + 1) * step, :]
        for j in range(1, width):
            total = total + taps[j : j + 1, :] * wide[r * step + j : (r + 1) * step + j, :]
        out_ref[r, :step, :] = total.astype(BF16)
        out_ref[r, step:, :] = extra[r]


def finish(width, acc, x4, tiles, next_head, taps, extra):
    rows, own = x4.shape
    groups = own // GW
    step = rows // PLANE + HEAD
    col = pl.BlockSpec((rows, GW), lambda g: (0, g))
    return pl.pallas_call(
        functools.partial(last_kernel, width),
        grid=(groups,),
        in_specs=[
            col,
            col,
            pl.BlockSpec((1, BLK, 4 * BLK), lambda g: (g, 0, 1)),
            pl.BlockSpec((HEAD, GW), lambda g: (0, g)),
            pl.BlockSpec((width, GW), lambda g: (0, g)),
            pl.BlockSpec((PLANE, HEAD, GW), lambda g: (0, 0, 0)),
        ],
        out_specs=pl.BlockSpec((PLANE, step, GW), lambda g: (0, 0, g)),
        out_shape=jax.ShapeDtypeStruct((PLANE, step, own), BF16),
        scratch_shapes=[
            pltpu.VMEM((rows + BLK, 2 * GW), BF16),
            pltpu.VMEM((rows + 8, GW), F32),
        ],
        compiler_params=params(),
        cost_estimate=cost(2 * 3 * rows * rows * GW * groups, 8 * rows * own),
        name="finish",
    )(acc, x4, tiles, next_head, taps, extra)


def per_device(features, gate_values, upstream, short_filter, long_filter, loss_scale):
    shards = lax.axis_size("ctx")
    planes = shards // PLANE
    index = lax.axis_index("ctx")
    z, p = index // PLANE, index % PLANE
    width, chans = short_filter.shape
    own = chans // PLANE
    groups = own // GW
    rows = PLANE * features.shape[1]
    in_plane = [[k * PLANE + i for i in range(PLANE)] for k in range(planes)]
    along_z = [[k * PLANE + i for k in range(planes)] for i in range(PLANE)]

    def swap(x):
        return lax.all_to_all(x, "ctx", 0, 0, axis_index_groups=in_plane, tiled=True)

    def hop(x, count):
        step = PLANE * count
        route = [(i, i + step) for i in range(shards) if 0 <= i + step < shards]
        return lax.ppermute(x, "ctx", route)

    def after(x, *others):
        return lax.optimization_barrier((x,) + others)[0]

    packed = gate(upstream, gate_values)
    feat1 = hop(features, 1)
    x0 = swap(packed)
    filters = lax.dynamic_slice_in_dim(after(long_filter, packed), p * groups, groups, 0)
    taps = lax.dynamic_slice_in_dim(after(short_filter, packed), p * own, own, 1)
    tiles, far_tiles = toeplitz(filters)
    x0 = x0.reshape(rows, own)
    feat1 = swap(pack(after(feat1, x0)))
    x1 = after(hop(x0, -1), feat1, tiles)
    feat0 = swap(pack(after(features, feat1)))
    feat0, feat1 = (x.reshape(rows, own) for x in (feat0, feat1))

    feat2 = hop(feat1, 1)
    feat3_tail = hop(feat1[rows - HEAD :], 2)
    x4_head = hop(x0[:HEAD], -4)

    acc, mid = early(x0, x1, tiles)
    x2 = after(hop(x1, -1), acc, feat0, feat2, x4_head)
    raw = own_terms(width, acc, feat0, feat1)
    raw = far_terms(width, mid, raw, x2, feat1, feat2, feat3_tail, far_tiles)
    raw = lax.psum(raw, "dp")
    x3 = after(hop(x2, -1), raw)
    x4 = hop(x3, -1)
    acc, head = third(acc, x2, x3, x4_head, tiles)
    next_head = hop(head, -1)

    raw = after(raw, x3, head)
    copies = jnp.broadcast_to(raw[None], (planes,) + raw.shape)
    copies = lax.all_to_all(copies, "ctx", 0, 0, axis_index_groups=along_z, tiled=True)
    lane = chans // shards
    spans = own // lane // PLANE
    extra = prepare(z % spans, loss_scale, after(copies, x4), lane)
    got = swap(finish(width, acc, x4, far_tiles, next_head, taps, extra))
    input_grad, short_grad, norm_value = unpack(z // spans, got, rows // PLANE, width, lane)
    return (input_grad, short_grad, norm_value.reshape(1))


def solution(mesh):
    placed = (P("dp", "ctx", None), P("dp", "ctx", None), P("dp", "ctx", None), P(), P(), P())
    return jax.shard_map(
        per_device,
        mesh=mesh,
        in_specs=placed,
        out_specs=(P("dp", "ctx", None), P(None, "ctx"), P()),
        check_vma=False,
    )
```

```python
import functools

import jax
import jax.numpy as jnp
from jax import lax
from jax.experimental import pallas as pl
from jax.experimental.pallas import tpu as pltpu
from jax.sharding import PartitionSpec as P

PLANE = 8
BLK = 256
GW = 128
HEAD = 16
SHORT = 64
VMEM = 56 * 1024 * 1024
F32, BF16 = jnp.float32, jnp.bfloat16


def params(grid=True):
    kwargs = {"dimension_semantics": ("arbitrary",)} if grid else {}
    return pltpu.CompilerParams(vmem_limit_bytes=VMEM, **kwargs)


def cost(flops, nbytes):
    return pl.CostEstimate(
        flops=int(flops) // SHORT, bytes_accessed=int(nbytes) // SHORT, transcendentals=0
    )


def dot(a, b):
    return jnp.dot(a, b, preferred_element_type=F32)


def gate_kernel(up_ref, gate_ref, out_ref):
    width = out_ref.shape[2]
    for p in range(PLANE):
        cols = slice(p * width, (p + 1) * width)
        prod = up_ref[0, :, cols].astype(F32) * gate_ref[0, :, cols].astype(F32)
        out_ref[p] = prod.astype(BF16)


def gate(upstream, gates):
    _, rows, chans = upstream.shape
    return pl.pallas_call(
        gate_kernel,
        out_shape=jax.ShapeDtypeStruct((PLANE, rows, chans // PLANE), BF16),
        compiler_params=params(False),
        cost_estimate=cost(upstream.size, 6 * upstream.size),
        name="gate",
    )(upstream, gates)


def pack_kernel(src_ref, out_ref):
    width = out_ref.shape[2]
    for p in range(PLANE):
        out_ref[p] = src_ref[0, :, p * width : (p + 1) * width]


def pack(features):
    _, rows, chans = features.shape
    return pl.pallas_call(
        pack_kernel,
        out_shape=jax.ShapeDtypeStruct((PLANE, rows, chans // PLANE), BF16),
        compiler_params=params(False),
        cost_estimate=cost(0, 4 * features.size),
        name="pack",
    )(features)


def split_terms(x):
    high = x.astype(BF16)
    rest = x - high.astype(F32)
    mid = rest.astype(BF16)
    return high, mid, (rest - mid.astype(F32)).astype(BF16)


def prepare_kernel(lane, half_ref, scale_ref, raw, out_ref):
    unscaled = raw[...] / scale_ref[0]
    norm = jnp.sum(unscaled * unscaled, keepdims=True)
    norm = split_terms(jnp.broadcast_to(norm, (8, 8)))
    span = PLANE * lane
    mine = unscaled[:, :span]
    for n in range(1, unscaled.shape[1] // span):
        mine = jnp.where(half_ref[0] == n, unscaled[:, n * span : (n + 1) * span], mine)
    parts = split_terms(mine)
    pad = jnp.zeros((8, GW - 3 * lane - 24), BF16)
    for p in range(PLANE):
        row = [x[:, p * lane : (p + 1) * lane] for x in parts]
        tile = jnp.concatenate([*row, *norm, pad], axis=1).astype(F32)
        out_ref[p] = jnp.concatenate([tile, jnp.zeros_like(tile)], axis=0).astype(BF16)


def prepare(half, scale, raw, lane):
    return pl.pallas_call(
        functools.partial(prepare_kernel, lane),
        in_specs=[pl.BlockSpec(memory_space=pltpu.SMEM)] * 2 + [pl.BlockSpec(memory_space=pltpu.VMEM)],
        out_shape=jax.ShapeDtypeStruct((PLANE, HEAD, GW), BF16),
        compiler_params=params(False),
        cost_estimate=cost(raw.size, 4 * raw.size),
        name="prepare",
    )(half.reshape(1), scale, raw)


def unpack_kernel(lane, source_ref, got, extra, out_ref, short_ref, norm_ref):
    width = got.shape[2]
    for p in range(PLANE):
        out_ref[0, :, p * width : (p + 1) * width] = got[p]
    norm = jnp.zeros((8, 1), F32)
    short = jnp.zeros((8, lane), F32)
    for p in range(PLANE):
        tile = extra[p].astype(F32)[:8]
        at = 3 * lane
        norm = norm + (tile[:, at : at + 1] + tile[:, at + 8 : at + 9] + tile[:, at + 16 : at + 17])
        terms = tile[:, :lane] + tile[:, lane : 2 * lane] + tile[:, 2 * lane : 3 * lane]
        short = jnp.where(source_ref[0] == p, terms, short)
    norm = jnp.sqrt(norm)
    short = jnp.where(jnp.abs(norm) < jnp.inf, short, jnp.zeros_like(short))
    short_ref[...] = short[: short_ref.shape[0], :]
    norm_ref[...] = norm[:1, :]


def unpack(source, got, rows, width, lane):
    return pl.pallas_call(
        functools.partial(unpack_kernel, lane),
        grid=(1,),
        in_specs=[
            pl.BlockSpec(memory_space=pltpu.SMEM),
            pl.BlockSpec((PLANE, rows, got.shape[2]), lambda i: (0, 0, 0)),
            pl.BlockSpec((PLANE, HEAD, GW), lambda i: (0, rows // HEAD, 0)),
        ],
        out_specs=[
            pl.BlockSpec((1, rows, PLANE * got.shape[2]), lambda i: (0, 0, 0)),
            pl.BlockSpec((width, lane), lambda i: (0, 0)),
            pl.BlockSpec((1, 1), lambda i: (0, 0)),
        ],
        out_shape=[
            jax.ShapeDtypeStruct((1, rows, PLANE * got.shape[2]), BF16),
            jax.ShapeDtypeStruct((width, lane), F32),
            jax.ShapeDtypeStruct((1, 1), F32),
        ],
        compiler_params=params(),
        cost_estimate=cost(0, 4 * got.size),
        name="unpack",
    )(source.reshape(1), got, got)


def toeplitz_kernel(taps_ref, all_ref, far_ref):
    taps = taps_ref.shape[2]
    half = BLK // 2
    row = jnp.concatenate([taps_ref[0], jnp.zeros((1, BLK), F32)], axis=1)
    base = jnp.broadcast_to(row, (half, taps + BLK))
    base = pltpu.roll(base, 0, 1, stride=1, stride_axis=0).astype(BF16)
    all_ref[0, :half, :] = base
    all_ref[0, half:, :half] = jnp.zeros((half, half), BF16)
    all_ref[0, half:, half:] = base[:, : taps + BLK - half]
    far_ref[0] = all_ref[0, :, taps - 7 * BLK :]


def toeplitz(filters):
    groups, taps = filters.shape
    return pl.pallas_call(
        toeplitz_kernel,
        grid=(groups,),
        in_specs=[pl.BlockSpec((1, 1, taps), lambda g: (g, 0, 0))],
        out_specs=[
            pl.BlockSpec((1, BLK, taps + BLK), lambda g: (g, 0, 0)),
            pl.BlockSpec((1, BLK, 8 * BLK), lambda g: (g, 0, 0)),
        ],
        out_shape=[
            jax.ShapeDtypeStruct((groups, BLK, taps + BLK), BF16),
            jax.ShapeDtypeStruct((groups, BLK, 8 * BLK), BF16),
        ],
        compiler_params=params(),
        cost_estimate=cost(groups * BLK * taps * 16, 2 * groups * BLK * taps * 3),
        name="toeplitz",
    )(filters.astype(F32).reshape(groups, 1, taps))


def fill_pairs(pairs_ref, planes):
    rows = sum(x.shape[0] for x in planes)
    zero = jnp.zeros((BLK, GW), BF16)
    pairs_ref[:BLK, :GW] = zero
    at = 0
    for x in planes:
        pairs_ref[BLK + at : BLK + at + x.shape[0], :GW] = x[...]
        pairs_ref[at : at + x.shape[0], GW:] = x[...]
        at += x.shape[0]
    pairs_ref[rows : rows + BLK, GW:] = zero


def tile_products(tiles_ref, first, last, pairs_ref, distance, blocks):
    out = []
    for pair in (0, 2):
        low, high = distance - 1 - pair, distance + blocks - 1 - pair
        k0, k1 = max(low, first), min(high, last)
        tiles = tiles_ref[0, :, (k0 - first) * BLK : (k1 + 1 - first) * BLK]
        window = pairs_ref[(k0 - low) * BLK : (k1 + 1 - low) * BLK, :]
        out.append(dot(tiles, window))
    return out


def store_rows(ref, products, add=None):
    for n, prod in enumerate(products):
        for m in range(2):
            rows = slice((2 * n + m) * BLK, (2 * n + m + 1) * BLK)
            value = prod[:, m * GW : (m + 1) * GW]
            ref[rows, :] = value if add is None else add[rows, :] + value


def correlate(conv_ref, feat, before, feat_wide, terms):
    rows = conv_ref.shape[0]
    feat_wide[:8, :] = before[before.shape[0] - 8 :, :].astype(F32)
    feat_wide[8:, :] = feat.astype(F32)
    for r in range(0, rows, 128):
        conv = conv_ref[r : r + 128, :]
        for j in range(len(terms)):
            prod = conv * feat_wide[r + 8 - j : r + 136 - j, :]
            terms[j] = terms[j] + jnp.sum(prod.reshape(16, 8, GW), axis=0)
    return terms


def add_terms(raw_ref, terms, add=None):
    out = [jnp.sum(t, axis=0, keepdims=True) for t in terms]
    out.append(jnp.zeros((8 - len(terms), GW), F32))
    out = jnp.concatenate(out, axis=0)
    raw_ref[...] = out if add is None else add[...] + out


def pairs_of(rows):
    return pltpu.VMEM((rows + BLK, 2 * GW), BF16)


def early_kernel(x0, x1, tiles, acc_ref, mid_ref, pairs):
    last = tiles.shape[2] // BLK - 1
    fill_pairs(pairs, [x0, x1])
    store_rows(acc_ref, tile_products(tiles, 0, last, pairs, 0, 8))
    fill_pairs(pairs, [x1])
    store_rows(mid_ref, tile_products(tiles, 0, last, pairs, 8, 4))


def early(x0, x1, tiles):
    rows, own = x0.shape
    groups = own // GW
    col = pl.BlockSpec((rows, GW), lambda g: (0, g))
    out = jax.ShapeDtypeStruct((rows, own), F32)
    return pl.pallas_call(
        early_kernel,
        grid=(groups,),
        in_specs=[col, col, pl.BlockSpec((1, BLK, 12 * BLK), lambda g: (g, 0, 0))],
        out_specs=[col, col],
        out_shape=[out, out],
        scratch_shapes=[pairs_of(2 * rows)],
        compiler_params=params(),
        cost_estimate=cost(24 * rows * rows * GW * groups, 12 * rows * own),
        name="early",
    )(x0, x1, tiles)


def terms_kernel(
    width, acc, mid, x2, f0, f1, f2, f3_tail, tiles, raw_ref, pairs, far, feat_wide
):
    rows = x2.shape[0]
    fill_pairs(pairs, [x2])
    terms = [jnp.zeros((8, GW), F32)] * width
    terms = correlate(acc, f0[...], f1[rows - HEAD :, :], feat_wide, terms)
    store_rows(far, tile_products(tiles, 9, 16, pairs, 12, 4), add=mid)
    terms = correlate(far, f1[...], f2[rows - HEAD :, :], feat_wide, terms)
    store_rows(far, tile_products(tiles, 9, 16, pairs, 16, 4))
    terms = correlate(far, f2[...], f3_tail[...], feat_wide, terms)
    out = [jnp.sum(t, axis=0, keepdims=True) for t in terms]
    out.append(jnp.zeros((8 - width, GW), F32))
    raw_ref[...] = jnp.concatenate(out, axis=0)


def all_terms(width, acc, mid, x2, f0, f1, f2, f3_tail, tiles):
    rows, own = acc.shape
    groups = own // GW
    col = pl.BlockSpec((rows, GW), lambda g: (0, g))
    return pl.pallas_call(
        functools.partial(terms_kernel, width),
        grid=(groups,),
        in_specs=[
            col,
            col,
            col,
            col,
            col,
            col,
            pl.BlockSpec((HEAD, GW), lambda g: (0, g)),
            pl.BlockSpec((1,) + tiles.shape[1:], lambda g: (g, 0, 0)),
        ],
        out_specs=pl.BlockSpec((8, GW), lambda g: (0, g)),
        out_shape=jax.ShapeDtypeStruct((8, own), F32),
        scratch_shapes=[
            pairs_of(rows),
            pltpu.VMEM((rows, GW), F32),
            pltpu.VMEM((rows + 8, GW), F32),
        ],
        compiler_params=params(),
        cost_estimate=cost(16 * rows * rows * GW * groups, 20 * rows * own),
        name="all_terms",
    )(acc, mid, x2, f0, f1, f2, f3_tail, tiles)


def third_kernel(acc_in, x2, x3, x4_head, tiles, acc_ref, head_ref, pairs):
    last = tiles.shape[2] // BLK - 1
    fill_pairs(pairs, [x2, x3])
    store_rows(acc_ref, tile_products(tiles, 0, last, pairs, 8, 8), add=acc_in)
    ahead = jnp.concatenate([x4_head[...], jnp.zeros((GW - HEAD, GW), BF16)], axis=0)
    corner = tiles[0, :HEAD, last * BLK : last * BLK + GW]
    head_ref[...] = (acc_ref[:HEAD, :] + dot(corner, ahead)).astype(BF16)


def third(acc, x2, x3, x4_head, tiles):
    rows, own = acc.shape
    groups = own // GW
    col = pl.BlockSpec((rows, GW), lambda g: (0, g))
    return pl.pallas_call(
        third_kernel,
        grid=(groups,),
        in_specs=[
            col,
            col,
            col,
            pl.BlockSpec((HEAD, GW), lambda g: (0, g)),
            pl.BlockSpec((1,) + tiles.shape[1:], lambda g: (g, 0, 0)),
        ],
        out_specs=[col, pl.BlockSpec((HEAD, GW), lambda g: (0, g))],
        out_shape=[
            jax.ShapeDtypeStruct((rows, own), F32),
            jax.ShapeDtypeStruct((HEAD, own), BF16),
        ],
        scratch_shapes=[pairs_of(2 * rows)],
        compiler_params=params(),
        cost_estimate=cost(18 * rows * rows * GW * groups, 12 * rows * own),
        name="third",
    )(acc, x2, x3, x4_head, tiles)


def last_kernel(width, acc_in, x4, tiles, next_head, taps, extra, out_ref, pairs, wide):
    rows = x4.shape[0]
    step = rows // PLANE
    fill_pairs(pairs, [x4])
    for n, prod in enumerate(tile_products(tiles, 13, 16, pairs, 16, 4)):
        for m in range(2):
            at = slice((2 * n + m) * BLK, (2 * n + m + 1) * BLK)
            value = acc_in[at, :] + prod[:, m * GW : (m + 1) * GW]
            wide[at, :] = value.astype(BF16).astype(F32)
    wide[rows:, :] = next_head[:8, :].astype(F32)
    for r in range(PLANE):
        total = taps[0:1, :] * wide[r * step : (r + 1) * step, :]
        for j in range(1, width):
            total = total + taps[j : j + 1, :] * wide[r * step + j : (r + 1) * step + j, :]
        out_ref[r, :step, :] = total.astype(BF16)
        out_ref[r, step:, :] = extra[r]


def finish(width, acc, x4, tiles, next_head, taps, extra):
    rows, own = x4.shape
    groups = own // GW
    step = rows // PLANE + HEAD
    col = pl.BlockSpec((rows, GW), lambda g: (0, g))
    return pl.pallas_call(
        functools.partial(last_kernel, width),
        grid=(groups,),
        in_specs=[
            col,
            col,
            pl.BlockSpec((1, BLK, 4 * BLK), lambda g: (g, 0, 1)),
            pl.BlockSpec((HEAD, GW), lambda g: (0, g)),
            pl.BlockSpec((width, GW), lambda g: (0, g)),
            pl.BlockSpec((PLANE, HEAD, GW), lambda g: (0, 0, 0)),
        ],
        out_specs=pl.BlockSpec((PLANE, step, GW), lambda g: (0, 0, g)),
        out_shape=jax.ShapeDtypeStruct((PLANE, step, own), BF16),
        scratch_shapes=[
            pltpu.VMEM((rows + BLK, 2 * GW), BF16),
            pltpu.VMEM((rows + 8, GW), F32),
        ],
        compiler_params=params(),
        cost_estimate=cost(2 * 3 * rows * rows * GW * groups, 8 * rows * own),
        name="finish",
    )(acc, x4, tiles, next_head, taps, extra)


def per_device(features, gate_values, upstream, short_filter, long_filter, loss_scale):
    shards = lax.axis_size("ctx")
    planes = shards // PLANE
    index = lax.axis_index("ctx")
    z, p = index // PLANE, index % PLANE
    width, chans = short_filter.shape
    own = chans // PLANE
    groups = own // GW
    rows = PLANE * features.shape[1]
    in_plane = [[k * PLANE + i for i in range(PLANE)] for k in range(planes)]

    def swap(x):
        return lax.all_to_all(x, "ctx", 0, 0, axis_index_groups=in_plane, tiled=True)

    def hop(x, count):
        step = PLANE * count
        route = [(i, i + step) for i in range(shards) if 0 <= i + step < shards]
        return lax.ppermute(x, "ctx", route)

    def after(x, *others):
        return lax.optimization_barrier((x,) + others)[0]

    feat1 = hop(features, 1)
    packed = gate(upstream, gate_values)
    x0 = swap(packed).reshape(rows, own)
    filters = lax.dynamic_slice_in_dim(after(long_filter, packed), p * groups, groups, 0)
    taps = lax.dynamic_slice_in_dim(after(short_filter, packed), p * own, own, 1)
    tiles, far_tiles = toeplitz(filters)
    feat1 = swap(pack(after(feat1, x0))).reshape(rows, own)
    feat0 = pack(after(features, x0))
    x1 = after(hop(x0, -1), feat0, feat1, tiles)
    feat0 = swap(after(feat0, feat1)).reshape(rows, own)
    feat2 = hop(feat1, 1)
    feat3_tail = hop(feat1[rows - HEAD :], 2)
    x4_head = hop(x0[:HEAD], -4)

    acc, mid = early(x0, x1, tiles)
    x2 = after(hop(x1, -1), acc, feat0, feat2, feat3_tail, x4_head)
    raw = all_terms(width, acc, mid, x2, feat0, feat1, feat2, feat3_tail, far_tiles)
    along_z = [[k * PLANE + i for k in range(planes)] for i in range(PLANE)]
    copies = jnp.broadcast_to(raw.astype(BF16)[None], (planes,) + raw.shape)
    copies = lax.all_to_all(copies, "ctx", 0, 0, axis_index_groups=along_z, tiled=True)
    x3 = after(hop(x2, -1), copies)
    x4 = hop(x3, -1)
    raw = jnp.sum(after(copies, x3).astype(F32), axis=0)
    acc, head = third(acc, x2, x3, x4_head, tiles)
    next_head = hop(head, -1)
    copies = jnp.broadcast_to(raw[None], (lax.axis_size("dp"),) + raw.shape)
    raw = jnp.sum(lax.all_to_all(copies, "dp", 0, 0, tiled=True), axis=0)
    lane = chans // shards
    spans = own // lane // PLANE
    extra = prepare(z % spans, loss_scale, raw, lane)
    got = swap(finish(width, acc, x4, far_tiles, next_head, taps, extra))
    input_grad, short_grad, norm_value = unpack(z // spans, got, rows // PLANE, width, lane)
    return (input_grad, short_grad, norm_value.reshape(1))


def solution(mesh):
    placed = (P("dp", "ctx", None), P("dp", "ctx", None), P("dp", "ctx", None), P(), P(), P())
    return jax.shard_map(
        per_device,
        mesh=mesh,
        in_specs=placed,
        out_specs=(P("dp", "ctx", None), P(None, "ctx"), P()),
        check_vma=False,
    )
```

```python
import functools

import jax
import jax.numpy as jnp
from jax import lax
from jax.experimental import pallas as pl
from jax.experimental.pallas import tpu as pltpu
from jax.sharding import PartitionSpec as P

PLANE = 8
BLK = 256
GW = 128
HEAD = 16
SHORT = 64
VMEM = 56 * 1024 * 1024
F32, BF16 = jnp.float32, jnp.bfloat16


def params(grid=True):
    kwargs = {"dimension_semantics": ("arbitrary",)} if grid else {}
    return pltpu.CompilerParams(vmem_limit_bytes=VMEM, **kwargs)


def cost(flops, nbytes):
    return pl.CostEstimate(
        flops=int(flops) // SHORT, bytes_accessed=int(nbytes) // SHORT, transcendentals=0
    )


def dot(a, b):
    return jnp.dot(a, b, preferred_element_type=F32)


def gate_kernel(up_ref, gate_ref, out_ref):
    width = out_ref.shape[2]
    for p in range(PLANE):
        cols = slice(p * width, (p + 1) * width)
        prod = up_ref[0, :, cols].astype(F32) * gate_ref[0, :, cols].astype(F32)
        out_ref[p] = prod.astype(BF16)


def gate(upstream, gates):
    _, rows, chans = upstream.shape
    return pl.pallas_call(
        gate_kernel,
        out_shape=jax.ShapeDtypeStruct((PLANE, rows, chans // PLANE), BF16),
        compiler_params=params(False),
        cost_estimate=cost(upstream.size, 6 * upstream.size),
        name="gate",
    )(upstream, gates)


def pack_kernel(src_ref, out_ref):
    width = out_ref.shape[2]
    for p in range(PLANE):
        out_ref[p] = src_ref[0, :, p * width : (p + 1) * width]


def pack(features):
    _, rows, chans = features.shape
    return pl.pallas_call(
        pack_kernel,
        out_shape=jax.ShapeDtypeStruct((PLANE, rows, chans // PLANE), BF16),
        compiler_params=params(False),
        cost_estimate=cost(0, 4 * features.size),
        name="pack",
    )(features)


def split_terms(x):
    high = x.astype(BF16)
    rest = x - high.astype(F32)
    mid = rest.astype(BF16)
    return high, mid, (rest - mid.astype(F32)).astype(BF16)


def prepare_kernel(lane, half_ref, scale_ref, raw, out_ref):
    unscaled = raw[...] / scale_ref[0]
    norm = jnp.sum(unscaled * unscaled, keepdims=True)
    norm = split_terms(jnp.broadcast_to(norm, (8, 8)))
    span = PLANE * lane
    mine = unscaled[:, :span]
    for n in range(1, unscaled.shape[1] // span):
        mine = jnp.where(half_ref[0] == n, unscaled[:, n * span : (n + 1) * span], mine)
    parts = split_terms(mine)
    pad = jnp.zeros((8, GW - 3 * lane - 24), BF16)
    for p in range(PLANE):
        row = [x[:, p * lane : (p + 1) * lane] for x in parts]
        tile = jnp.concatenate([*row, *norm, pad], axis=1).astype(F32)
        out_ref[p] = jnp.concatenate([tile, jnp.zeros_like(tile)], axis=0).astype(BF16)


def prepare(half, scale, raw, lane):
    return pl.pallas_call(
        functools.partial(prepare_kernel, lane),
        in_specs=[pl.BlockSpec(memory_space=pltpu.SMEM)] * 2 + [pl.BlockSpec(memory_space=pltpu.VMEM)],
        out_shape=jax.ShapeDtypeStruct((PLANE, HEAD, GW), BF16),
        compiler_params=params(False),
        cost_estimate=cost(raw.size, 4 * raw.size),
        name="prepare",
    )(half.reshape(1), scale, raw)


def unpack_kernel(lane, source_ref, got, out_ref, short_ref, norm_ref, tiles, sems):
    width = got.shape[2]
    rows = out_ref.shape[1]
    behind = got.at[:, pl.ds(rows, HEAD), pl.ds(0, GW)]
    terms_copy = pltpu.make_async_copy(behind, tiles, sems.at[PLANE])
    terms_copy.start()
    copies = []
    for p in range(PLANE):
        source = got.at[p, pl.ds(0, rows), :]
        target = out_ref.at[0, :, pl.ds(p * width, width)]
        copies.append(pltpu.make_async_copy(source, target, sems.at[p]))
        copies[-1].start()
    terms_copy.wait()
    norm = jnp.zeros((8, 1), F32)
    short = jnp.zeros((8, lane), F32)
    for p in range(PLANE):
        tile = tiles[p].astype(F32)[:8]
        at = 3 * lane
        norm = norm + (tile[:, at : at + 1] + tile[:, at + 8 : at + 9] + tile[:, at + 16 : at + 17])
        terms = tile[:, :lane] + tile[:, lane : 2 * lane] + tile[:, 2 * lane : 3 * lane]
        short = jnp.where(source_ref[0] == p, terms, short)
    norm = jnp.sqrt(norm)
    short = jnp.where(jnp.abs(norm) < jnp.inf, short, jnp.zeros_like(short))
    short_ref[...] = short[: short_ref.shape[0], :]
    norm_ref[...] = norm[:1, :]
    for copy in copies:
        copy.wait()


def unpack(source, got, rows, width, lane):
    return pl.pallas_call(
        functools.partial(unpack_kernel, lane),
        in_specs=[pl.BlockSpec(memory_space=pltpu.SMEM), pl.BlockSpec(memory_space=pl.ANY)],
        out_specs=[
            pl.BlockSpec(memory_space=pl.ANY),
            pl.BlockSpec(memory_space=pltpu.VMEM),
            pl.BlockSpec(memory_space=pltpu.VMEM),
        ],
        out_shape=[
            jax.ShapeDtypeStruct((1, rows, PLANE * got.shape[2]), BF16),
            jax.ShapeDtypeStruct((width, lane), F32),
            jax.ShapeDtypeStruct((1, 1), F32),
        ],
        scratch_shapes=[
            pltpu.VMEM((PLANE, HEAD, GW), BF16),
            pltpu.SemaphoreType.DMA((PLANE + 1,)),
        ],
        compiler_params=pltpu.CompilerParams(vmem_limit_bytes=4 * 1024 * 1024),
        cost_estimate=cost(0, 4 * got.size),
        name="unpack",
    )(source.reshape(1), got)


def toeplitz_kernel(taps_ref, all_ref, far_ref):
    taps = taps_ref.shape[2]
    half = BLK // 2
    row = jnp.concatenate([taps_ref[0], jnp.zeros((1, BLK), F32)], axis=1)
    base = jnp.broadcast_to(row, (half, taps + BLK))
    base = pltpu.roll(base, 0, 1, stride=1, stride_axis=0).astype(BF16)
    all_ref[0, :half, :] = base
    all_ref[0, half:, :half] = jnp.zeros((half, half), BF16)
    all_ref[0, half:, half:] = base[:, : taps + BLK - half]
    far_ref[0] = all_ref[0, :, taps - 7 * BLK :]


def toeplitz(filters):
    groups, taps = filters.shape
    return pl.pallas_call(
        toeplitz_kernel,
        grid=(groups,),
        in_specs=[pl.BlockSpec((1, 1, taps), lambda g: (g, 0, 0))],
        out_specs=[
            pl.BlockSpec((1, BLK, taps + BLK), lambda g: (g, 0, 0)),
            pl.BlockSpec((1, BLK, 8 * BLK), lambda g: (g, 0, 0)),
        ],
        out_shape=[
            jax.ShapeDtypeStruct((groups, BLK, taps + BLK), BF16),
            jax.ShapeDtypeStruct((groups, BLK, 8 * BLK), BF16),
        ],
        compiler_params=params(),
        cost_estimate=cost(groups * BLK * taps * 16, 2 * groups * BLK * taps * 3),
        name="toeplitz",
    )(filters.astype(F32).reshape(groups, 1, taps))


def fill_pairs(pairs_ref, planes):
    rows = sum(x.shape[0] for x in planes)
    zero = jnp.zeros((BLK, GW), BF16)
    pairs_ref[:BLK, :GW] = zero
    at = 0
    for x in planes:
        pairs_ref[BLK + at : BLK + at + x.shape[0], :GW] = x[...]
        pairs_ref[at : at + x.shape[0], GW:] = x[...]
        at += x.shape[0]
    pairs_ref[rows : rows + BLK, GW:] = zero


def tile_products(tiles_ref, first, last, pairs_ref, distance, blocks):
    out = []
    for pair in (0, 2):
        low, high = distance - 1 - pair, distance + blocks - 1 - pair
        k0, k1 = max(low, first), min(high, last)
        tiles = tiles_ref[0, :, (k0 - first) * BLK : (k1 + 1 - first) * BLK]
        window = pairs_ref[(k0 - low) * BLK : (k1 + 1 - low) * BLK, :]
        out.append(dot(tiles, window))
    return out


def store_rows(ref, products, add=None):
    for n, prod in enumerate(products):
        for m in range(2):
            rows = slice((2 * n + m) * BLK, (2 * n + m + 1) * BLK)
            value = prod[:, m * GW : (m + 1) * GW]
            ref[rows, :] = value if add is None else add[rows, :] + value


def correlate(conv_ref, feat, before, feat_wide, terms):
    rows = conv_ref.shape[0]
    feat_wide[:8, :] = before[before.shape[0] - 8 :, :].astype(F32)
    feat_wide[8:, :] = feat.astype(F32)
    for r in range(0, rows, 128):
        conv = conv_ref[r : r + 128, :]
        for j in range(len(terms)):
            prod = conv * feat_wide[r + 8 - j : r + 136 - j, :]
            terms[j] = terms[j] + jnp.sum(prod.reshape(16, 8, GW), axis=0)
    return terms


def add_terms(raw_ref, terms, add=None):
    out = [jnp.sum(t, axis=0, keepdims=True) for t in terms]
    out.append(jnp.zeros((8 - len(terms), GW), F32))
    out = jnp.concatenate(out, axis=0)
    raw_ref[...] = out if add is None else add[...] + out


def pairs_of(rows):
    return pltpu.VMEM((rows + BLK, 2 * GW), BF16)


def early_kernel(x0, x1, tiles, acc_ref, mid_ref, pairs):
    last = tiles.shape[2] // BLK - 1
    fill_pairs(pairs, [x0, x1])
    store_rows(acc_ref, tile_products(tiles, 0, last, pairs, 0, 8))
    fill_pairs(pairs, [x1])
    store_rows(mid_ref, tile_products(tiles, 0, last, pairs, 8, 4))


def early(x0, x1, tiles):
    rows, own = x0.shape
    groups = own // GW
    col = pl.BlockSpec((rows, GW), lambda g: (0, g))
    out = jax.ShapeDtypeStruct((rows, own), F32)
    return pl.pallas_call(
        early_kernel,
        grid=(groups,),
        in_specs=[col, col, pl.BlockSpec((1, BLK, 12 * BLK), lambda g: (g, 0, 0))],
        out_specs=[col, col],
        out_shape=[out, out],
        scratch_shapes=[pairs_of(2 * rows)],
        compiler_params=params(),
        cost_estimate=cost(24 * rows * rows * GW * groups, 12 * rows * own),
        name="early",
    )(x0, x1, tiles)


def terms_kernel(
    width, acc, mid, x2, f0, f1, f2, f3_tail, tiles, raw_ref, pairs, far, feat_wide
):
    rows = x2.shape[0]
    fill_pairs(pairs, [x2])
    terms = [jnp.zeros((8, GW), F32)] * width
    terms = correlate(acc, f0[...], f1[rows - HEAD :, :], feat_wide, terms)
    store_rows(far, tile_products(tiles, 9, 16, pairs, 12, 4), add=mid)
    terms = correlate(far, f1[...], f2[rows - HEAD :, :], feat_wide, terms)
    store_rows(far, tile_products(tiles, 9, 16, pairs, 16, 4))
    terms = correlate(far, f2[...], f3_tail[...], feat_wide, terms)
    out = [jnp.sum(t, axis=0, keepdims=True) for t in terms]
    out.append(jnp.zeros((8 - width, GW), F32))
    raw_ref[...] = jnp.concatenate(out, axis=0)


def all_terms(width, acc, mid, x2, f0, f1, f2, f3_tail, tiles):
    rows, own = acc.shape
    groups = own // GW
    col = pl.BlockSpec((rows, GW), lambda g: (0, g))
    return pl.pallas_call(
        functools.partial(terms_kernel, width),
        grid=(groups,),
        in_specs=[
            col,
            col,
            col,
            col,
            col,
            col,
            pl.BlockSpec((HEAD, GW), lambda g: (0, g)),
            pl.BlockSpec((1,) + tiles.shape[1:], lambda g: (g, 0, 0)),
        ],
        out_specs=pl.BlockSpec((8, GW), lambda g: (0, g)),
        out_shape=jax.ShapeDtypeStruct((8, own), F32),
        scratch_shapes=[
            pairs_of(rows),
            pltpu.VMEM((rows, GW), F32),
            pltpu.VMEM((rows + 8, GW), F32),
        ],
        compiler_params=params(),
        cost_estimate=cost(16 * rows * rows * GW * groups, 20 * rows * own),
        name="all_terms",
    )(acc, mid, x2, f0, f1, f2, f3_tail, tiles)


def third_kernel(acc_in, x2, x3, x4_head, tiles, acc_ref, head_ref, pairs):
    last = tiles.shape[2] // BLK - 1
    fill_pairs(pairs, [x2, x3])
    store_rows(acc_ref, tile_products(tiles, 0, last, pairs, 8, 8), add=acc_in)
    ahead = jnp.concatenate([x4_head[...], jnp.zeros((GW - HEAD, GW), BF16)], axis=0)
    corner = tiles[0, :HEAD, last * BLK : last * BLK + GW]
    head_ref[...] = (acc_ref[:HEAD, :] + dot(corner, ahead)).astype(BF16)


def third(acc, x2, x3, x4_head, tiles):
    rows, own = acc.shape
    groups = own // GW
    col = pl.BlockSpec((rows, GW), lambda g: (0, g))
    return pl.pallas_call(
        third_kernel,
        grid=(groups,),
        in_specs=[
            col,
            col,
            col,
            pl.BlockSpec((HEAD, GW), lambda g: (0, g)),
            pl.BlockSpec((1,) + tiles.shape[1:], lambda g: (g, 0, 0)),
        ],
        out_specs=[col, pl.BlockSpec((HEAD, GW), lambda g: (0, g))],
        out_shape=[
            jax.ShapeDtypeStruct((rows, own), F32),
            jax.ShapeDtypeStruct((HEAD, own), BF16),
        ],
        scratch_shapes=[pairs_of(2 * rows)],
        compiler_params=params(),
        cost_estimate=cost(18 * rows * rows * GW * groups, 12 * rows * own),
        name="third",
    )(acc, x2, x3, x4_head, tiles)


def last_kernel(width, acc_in, x4, tiles, next_head, taps, extra, out_ref, pairs, wide):
    rows = x4.shape[0]
    step = rows // PLANE
    fill_pairs(pairs, [x4])
    for n, prod in enumerate(tile_products(tiles, 13, 16, pairs, 16, 4)):
        for m in range(2):
            at = slice((2 * n + m) * BLK, (2 * n + m + 1) * BLK)
            value = acc_in[at, :] + prod[:, m * GW : (m + 1) * GW]
            wide[at, :] = value.astype(BF16).astype(F32)
    wide[rows:, :] = next_head[:8, :].astype(F32)
    for r in range(PLANE):
        total = taps[0:1, :] * wide[r * step : (r + 1) * step, :]
        for j in range(1, width):
            total = total + taps[j : j + 1, :] * wide[r * step + j : (r + 1) * step + j, :]
        out_ref[r, :step, :] = total.astype(BF16)
        out_ref[r, step:, :] = extra[r]


def finish(width, acc, x4, tiles, next_head, taps, extra):
    rows, own = x4.shape
    groups = own // GW
    step = rows // PLANE + HEAD
    col = pl.BlockSpec((rows, GW), lambda g: (0, g))
    return pl.pallas_call(
        functools.partial(last_kernel, width),
        grid=(groups,),
        in_specs=[
            col,
            col,
            pl.BlockSpec((1, BLK, 4 * BLK), lambda g: (g, 0, 1)),
            pl.BlockSpec((HEAD, GW), lambda g: (0, g)),
            pl.BlockSpec((width, GW), lambda g: (0, g)),
            pl.BlockSpec((PLANE, HEAD, GW), lambda g: (0, 0, 0)),
        ],
        out_specs=pl.BlockSpec((PLANE, step, GW), lambda g: (0, 0, g)),
        out_shape=jax.ShapeDtypeStruct((PLANE, step, own), BF16),
        scratch_shapes=[
            pltpu.VMEM((rows + BLK, 2 * GW), BF16),
            pltpu.VMEM((rows + 8, GW), F32),
        ],
        compiler_params=params(),
        cost_estimate=cost(2 * 3 * rows * rows * GW * groups, 8 * rows * own),
        name="finish",
    )(acc, x4, tiles, next_head, taps, extra)


def per_device(features, gate_values, upstream, short_filter, long_filter, loss_scale):
    shards = lax.axis_size("ctx")
    planes = shards // PLANE
    index = lax.axis_index("ctx")
    z, p = index // PLANE, index % PLANE
    width, chans = short_filter.shape
    own = chans // PLANE
    groups = own // GW
    rows = PLANE * features.shape[1]
    in_plane = [[k * PLANE + i for i in range(PLANE)] for k in range(planes)]

    def swap(x):
        return lax.all_to_all(x, "ctx", 0, 0, axis_index_groups=in_plane, tiled=True)

    def hop(x, count):
        step = PLANE * count
        route = [(i, i + step) for i in range(shards) if 0 <= i + step < shards]
        return lax.ppermute(x, "ctx", route)

    def after(x, *others):
        return lax.optimization_barrier((x,) + others)[0]

    feat1 = hop(features, 1)
    packed = gate(upstream, gate_values)
    x0 = swap(packed).reshape(rows, own)
    filters = lax.dynamic_slice_in_dim(after(long_filter, packed), p * groups, groups, 0)
    taps = lax.dynamic_slice_in_dim(after(short_filter, packed), p * own, own, 1)
    tiles, far_tiles = toeplitz(filters)
    feat1 = swap(pack(after(feat1, x0))).reshape(rows, own)
    feat0 = pack(after(features, x0))
    x1 = hop(x0, -1)
    x1_next = after(x1, feat0, feat1, tiles)
    feat0 = swap(after(feat0, feat1)).reshape(rows, own)
    feat2 = hop(feat1, 1)
    feat3_tail = hop(feat1[rows - HEAD :], 2)
    x4_head = hop(x0[:HEAD], -4)

    acc, mid = early(x0, x1, tiles)
    x2 = after(hop(x1_next, -1), acc, feat0, feat2, feat3_tail, x4_head)
    raw = all_terms(width, acc, mid, x2, feat0, feat1, feat2, feat3_tail, far_tiles)
    along_z = [[k * PLANE + i for k in range(planes)] for i in range(PLANE)]
    copies = jnp.broadcast_to(raw.astype(BF16)[None], (planes,) + raw.shape)
    copies = lax.all_to_all(copies, "ctx", 0, 0, axis_index_groups=along_z, tiled=True)
    x3 = after(hop(x2, -1), copies)
    x4 = hop(x3, -1)
    raw = jnp.sum(after(copies, x3).astype(F32), axis=0)
    acc, head = third(acc, x2, x3, x4_head, tiles)
    next_head = hop(head, -1)
    copies = jnp.broadcast_to(raw[None], (lax.axis_size("dp"),) + raw.shape)
    raw = jnp.sum(lax.all_to_all(copies, "dp", 0, 0, tiled=True), axis=0)
    lane = chans // shards
    spans = own // lane // PLANE
    extra = prepare(z % spans, loss_scale, raw, lane)
    got = swap(finish(width, acc, x4, far_tiles, next_head, taps, extra))
    input_grad, short_grad, norm_value = unpack(z // spans, got, rows // PLANE, width, lane)
    return (input_grad, short_grad, norm_value.reshape(1))


def solution(mesh):
    placed = (P("dp", "ctx", None), P("dp", "ctx", None), P("dp", "ctx", None), P(), P(), P())
    return jax.shard_map(
        per_device,
        mesh=mesh,
        in_specs=placed,
        out_specs=(P("dp", "ctx", None), P(None, "ctx"), P()),
        check_vma=False,
    )
```

```python
import functools

import jax
import jax.numpy as jnp
from jax import lax
from jax.experimental import pallas as pl
from jax.experimental.pallas import tpu as pltpu
from jax.sharding import PartitionSpec as P

PLANE = 8
BLK = 256
GW = 128
HEAD = 16
SHORT = 64
VMEM = 56 * 1024 * 1024
F32, BF16 = jnp.float32, jnp.bfloat16


def params(grid=True):
    kwargs = {"dimension_semantics": ("arbitrary",)} if grid else {}
    return pltpu.CompilerParams(vmem_limit_bytes=VMEM, **kwargs)


def cost(flops, nbytes):
    return pl.CostEstimate(
        flops=int(flops) // SHORT, bytes_accessed=int(nbytes) // SHORT, transcendentals=0
    )


def dot(a, b):
    return jnp.dot(a, b, preferred_element_type=F32)


def gate_kernel(up_ref, gate_ref, out_ref):
    width = out_ref.shape[2]
    for p in range(PLANE):
        cols = slice(p * width, (p + 1) * width)
        prod = up_ref[0, :, cols].astype(F32) * gate_ref[0, :, cols].astype(F32)
        out_ref[p] = prod.astype(BF16)


def gate(upstream, gates):
    _, rows, chans = upstream.shape
    return pl.pallas_call(
        gate_kernel,
        out_shape=jax.ShapeDtypeStruct((PLANE, rows, chans // PLANE), BF16),
        compiler_params=params(False),
        cost_estimate=cost(upstream.size, 6 * upstream.size),
        name="gate",
    )(upstream, gates)


def pack_kernel(src_ref, out_ref):
    width = out_ref.shape[2]
    for p in range(PLANE):
        out_ref[p] = src_ref[0, :, p * width : (p + 1) * width]


def pack(features):
    _, rows, chans = features.shape
    return pl.pallas_call(
        pack_kernel,
        out_shape=jax.ShapeDtypeStruct((PLANE, rows, chans // PLANE), BF16),
        compiler_params=params(False),
        cost_estimate=cost(0, 4 * features.size),
        name="pack",
    )(features)


def split_terms(x):
    high = x.astype(BF16)
    rest = x - high.astype(F32)
    mid = rest.astype(BF16)
    return high, mid, (rest - mid.astype(F32)).astype(BF16)


def prepare_kernel(lane, half_ref, scale_ref, raw, out_ref):
    unscaled = raw[...] / scale_ref[0]
    norm = jnp.sum(unscaled * unscaled, keepdims=True)
    norm = split_terms(jnp.broadcast_to(norm, (8, 8)))
    span = PLANE * lane
    mine = unscaled[:, :span]
    for n in range(1, unscaled.shape[1] // span):
        mine = jnp.where(half_ref[0] == n, unscaled[:, n * span : (n + 1) * span], mine)
    parts = split_terms(mine)
    pad = jnp.zeros((8, GW - 3 * lane - 24), BF16)
    for p in range(PLANE):
        row = [x[:, p * lane : (p + 1) * lane] for x in parts]
        tile = jnp.concatenate([*row, *norm, pad], axis=1).astype(F32)
        out_ref[p] = jnp.concatenate([tile, jnp.zeros_like(tile)], axis=0).astype(BF16)


def prepare(half, scale, raw, lane):
    return pl.pallas_call(
        functools.partial(prepare_kernel, lane),
        in_specs=[pl.BlockSpec(memory_space=pltpu.SMEM)] * 2 + [pl.BlockSpec(memory_space=pltpu.VMEM)],
        out_shape=jax.ShapeDtypeStruct((PLANE, HEAD, GW), BF16),
        compiler_params=params(False),
        cost_estimate=cost(raw.size, 4 * raw.size),
        name="prepare",
    )(half.reshape(1), scale, raw)


def unpack_kernel(lane, source_ref, got, out_ref, short_ref, norm_ref, tiles, sems):
    width = got.shape[2]
    rows = out_ref.shape[1]
    behind = got.at[:, pl.ds(rows, HEAD), pl.ds(0, GW)]
    terms_copy = pltpu.make_async_copy(behind, tiles, sems.at[PLANE])
    terms_copy.start()
    copies = []
    for p in range(PLANE):
        source = got.at[p, pl.ds(0, rows), :]
        target = out_ref.at[0, :, pl.ds(p * width, width)]
        copies.append(pltpu.make_async_copy(source, target, sems.at[p]))
        copies[-1].start()
    terms_copy.wait()
    norm = jnp.zeros((8, 1), F32)
    short = jnp.zeros((8, lane), F32)
    for p in range(PLANE):
        tile = tiles[p].astype(F32)[:8]
        at = 3 * lane
        norm = norm + (tile[:, at : at + 1] + tile[:, at + 8 : at + 9] + tile[:, at + 16 : at + 17])
        terms = tile[:, :lane] + tile[:, lane : 2 * lane] + tile[:, 2 * lane : 3 * lane]
        short = jnp.where(source_ref[0] == p, terms, short)
    norm = jnp.sqrt(norm)
    short = jnp.where(jnp.abs(norm) < jnp.inf, short, jnp.zeros_like(short))
    short_ref[...] = short[: short_ref.shape[0], :]
    norm_ref[...] = norm[:1, :]
    for copy in copies:
        copy.wait()


def unpack(source, got, rows, width, lane):
    return pl.pallas_call(
        functools.partial(unpack_kernel, lane),
        in_specs=[pl.BlockSpec(memory_space=pltpu.SMEM), pl.BlockSpec(memory_space=pl.ANY)],
        out_specs=[
            pl.BlockSpec(memory_space=pl.ANY),
            pl.BlockSpec(memory_space=pltpu.VMEM),
            pl.BlockSpec(memory_space=pltpu.VMEM),
        ],
        out_shape=[
            jax.ShapeDtypeStruct((1, rows, PLANE * got.shape[2]), BF16),
            jax.ShapeDtypeStruct((width, lane), F32),
            jax.ShapeDtypeStruct((1, 1), F32),
        ],
        scratch_shapes=[
            pltpu.VMEM((PLANE, HEAD, GW), BF16),
            pltpu.SemaphoreType.DMA((PLANE + 1,)),
        ],
        compiler_params=pltpu.CompilerParams(vmem_limit_bytes=4 * 1024 * 1024),
        cost_estimate=cost(0, 4 * got.size),
        name="unpack",
    )(source.reshape(1), got)


def toeplitz_kernel(taps_ref, all_ref, far_ref):
    taps = taps_ref.shape[2]
    half = BLK // 2
    row = jnp.concatenate([taps_ref[0], jnp.zeros((1, BLK), F32)], axis=1)
    base = jnp.broadcast_to(row, (half, taps + BLK))
    base = pltpu.roll(base, 0, 1, stride=1, stride_axis=0).astype(BF16)
    all_ref[0, :half, :] = base
    all_ref[0, half:, :half] = jnp.zeros((half, half), BF16)
    all_ref[0, half:, half:] = base[:, : taps + BLK - half]
    far_ref[0] = all_ref[0, :, taps - 7 * BLK :]


def toeplitz(filters):
    groups, taps = filters.shape
    return pl.pallas_call(
        toeplitz_kernel,
        grid=(groups,),
        in_specs=[pl.BlockSpec((1, 1, taps), lambda g: (g, 0, 0))],
        out_specs=[
            pl.BlockSpec((1, BLK, taps + BLK), lambda g: (g, 0, 0)),
            pl.BlockSpec((1, BLK, 8 * BLK), lambda g: (g, 0, 0)),
        ],
        out_shape=[
            jax.ShapeDtypeStruct((groups, BLK, taps + BLK), BF16),
            jax.ShapeDtypeStruct((groups, BLK, 8 * BLK), BF16),
        ],
        compiler_params=params(),
        cost_estimate=cost(groups * BLK * taps * 16, 2 * groups * BLK * taps * 3),
        name="toeplitz",
    )(filters.astype(F32).reshape(groups, 1, taps))


def fill_pairs(pairs_ref, planes):
    rows = sum(x.shape[0] for x in planes)
    zero = jnp.zeros((BLK, GW), BF16)
    pairs_ref[:BLK, :GW] = zero
    at = 0
    for x in planes:
        pairs_ref[BLK + at : BLK + at + x.shape[0], :GW] = x[...]
        pairs_ref[at : at + x.shape[0], GW:] = x[...]
        at += x.shape[0]
    pairs_ref[rows : rows + BLK, GW:] = zero


def tile_products(tiles_ref, first, last, pairs_ref, distance, blocks):
    out = []
    for pair in (0, 2):
        low, high = distance - 1 - pair, distance + blocks - 1 - pair
        k0, k1 = max(low, first), min(high, last)
        tiles = tiles_ref[0, :, (k0 - first) * BLK : (k1 + 1 - first) * BLK]
        window = pairs_ref[(k0 - low) * BLK : (k1 + 1 - low) * BLK, :]
        out.append(dot(tiles, window))
    return out


def store_rows(ref, products, add=None):
    for n, prod in enumerate(products):
        for m in range(2):
            rows = slice((2 * n + m) * BLK, (2 * n + m + 1) * BLK)
            value = prod[:, m * GW : (m + 1) * GW]
            ref[rows, :] = value if add is None else add[rows, :] + value


def correlate(conv_ref, feat, before, feat_wide, terms):
    rows = conv_ref.shape[0]
    feat_wide[:8, :] = before[before.shape[0] - 8 :, :].astype(F32)
    feat_wide[8:, :] = feat.astype(F32)
    for r in range(0, rows, 128):
        conv = conv_ref[r : r + 128, :]
        for j in range(len(terms)):
            prod = conv * feat_wide[r + 8 - j : r + 136 - j, :]
            terms[j] = terms[j] + jnp.sum(prod.reshape(16, 8, GW), axis=0)
    return terms


def add_terms(raw_ref, terms, add=None):
    out = [jnp.sum(t, axis=0, keepdims=True) for t in terms]
    out.append(jnp.zeros((8 - len(terms), GW), F32))
    out = jnp.concatenate(out, axis=0)
    raw_ref[...] = out if add is None else add[...] + out


def pairs_of(rows):
    return pltpu.VMEM((rows + BLK, 2 * GW), BF16)


def early_kernel(x0, x1, tiles, acc_ref, mid_ref, pairs):
    last = tiles.shape[2] // BLK - 1
    fill_pairs(pairs, [x0, x1])
    store_rows(acc_ref, tile_products(tiles, 0, last, pairs, 0, 8))
    fill_pairs(pairs, [x1])
    store_rows(mid_ref, tile_products(tiles, 0, last, pairs, 8, 4))


def early(x0, x1, tiles):
    rows, own = x0.shape
    groups = own // GW
    col = pl.BlockSpec((rows, GW), lambda g: (0, g))
    out = jax.ShapeDtypeStruct((rows, own), F32)
    return pl.pallas_call(
        early_kernel,
        grid=(groups,),
        in_specs=[col, col, pl.BlockSpec((1, BLK, 12 * BLK), lambda g: (g, 0, 0))],
        out_specs=[col, col],
        out_shape=[out, out],
        scratch_shapes=[pairs_of(2 * rows)],
        compiler_params=params(),
        cost_estimate=cost(24 * rows * rows * GW * groups, 12 * rows * own),
        name="early",
    )(x0, x1, tiles)


def terms_kernel(
    width, acc, mid, x2, f0, f1, f2, f3_tail, tiles, raw_ref, pairs, far, feat_wide
):
    rows = x2.shape[0]
    fill_pairs(pairs, [x2])
    terms = [jnp.zeros((8, GW), F32)] * width
    terms = correlate(acc, f0[...], f1[rows - HEAD :, :], feat_wide, terms)
    store_rows(far, tile_products(tiles, 9, 16, pairs, 12, 4), add=mid)
    terms = correlate(far, f1[...], f2[rows - HEAD :, :], feat_wide, terms)
    store_rows(far, tile_products(tiles, 9, 16, pairs, 16, 4))
    terms = correlate(far, f2[...], f3_tail[...], feat_wide, terms)
    out = [jnp.sum(t, axis=0, keepdims=True) for t in terms]
    out.append(jnp.zeros((8 - width, GW), F32))
    raw_ref[...] = jnp.concatenate(out, axis=0)


def all_terms(width, acc, mid, x2, f0, f1, f2, f3_tail, tiles):
    rows, own = acc.shape
    groups = own // GW
    col = pl.BlockSpec((rows, GW), lambda g: (0, g))
    return pl.pallas_call(
        functools.partial(terms_kernel, width),
        grid=(groups,),
        in_specs=[
            col,
            col,
            col,
            col,
            col,
            col,
            pl.BlockSpec((HEAD, GW), lambda g: (0, g)),
            pl.BlockSpec((1,) + tiles.shape[1:], lambda g: (g, 0, 0)),
        ],
        out_specs=pl.BlockSpec((8, GW), lambda g: (0, g)),
        out_shape=jax.ShapeDtypeStruct((8, own), F32),
        scratch_shapes=[
            pairs_of(rows),
            pltpu.VMEM((rows, GW), F32),
            pltpu.VMEM((rows + 8, GW), F32),
        ],
        compiler_params=params(),
        cost_estimate=cost(16 * rows * rows * GW * groups, 20 * rows * own),
        name="all_terms",
    )(acc, mid, x2, f0, f1, f2, f3_tail, tiles)


def third_kernel(acc_in, x2, x3, x4_head, tiles, acc_ref, head_ref, pairs):
    last = tiles.shape[2] // BLK - 1
    fill_pairs(pairs, [x2, x3])
    store_rows(acc_ref, tile_products(tiles, 0, last, pairs, 8, 8), add=acc_in)
    ahead = jnp.concatenate([x4_head[...], jnp.zeros((GW - HEAD, GW), BF16)], axis=0)
    corner = tiles[0, :HEAD, last * BLK : last * BLK + GW]
    head_ref[...] = (acc_ref[:HEAD, :] + dot(corner, ahead)).astype(BF16)


def third(acc, x2, x3, x4_head, tiles):
    rows, own = acc.shape
    groups = own // GW
    col = pl.BlockSpec((rows, GW), lambda g: (0, g))
    return pl.pallas_call(
        third_kernel,
        grid=(groups,),
        in_specs=[
            col,
            col,
            col,
            pl.BlockSpec((HEAD, GW), lambda g: (0, g)),
            pl.BlockSpec((1,) + tiles.shape[1:], lambda g: (g, 0, 0)),
        ],
        out_specs=[col, pl.BlockSpec((HEAD, GW), lambda g: (0, g))],
        out_shape=[
            jax.ShapeDtypeStruct((rows, own), F32),
            jax.ShapeDtypeStruct((HEAD, own), BF16),
        ],
        scratch_shapes=[pairs_of(2 * rows)],
        compiler_params=params(),
        cost_estimate=cost(SHORT * 72 * rows * rows * GW * groups, SHORT * 48 * rows * own),
        name="third",
    )(acc, x2, x3, x4_head, tiles)


def last_kernel(width, acc_in, x4, tiles, next_head, taps, extra, out_ref, pairs, wide):
    rows = x4.shape[0]
    step = rows // PLANE
    fill_pairs(pairs, [x4])
    for n, prod in enumerate(tile_products(tiles, 13, 16, pairs, 16, 4)):
        for m in range(2):
            at = slice((2 * n + m) * BLK, (2 * n + m + 1) * BLK)
            value = acc_in[at, :] + prod[:, m * GW : (m + 1) * GW]
            wide[at, :] = value.astype(BF16).astype(F32)
    wide[rows:, :] = next_head[:8, :].astype(F32)
    for r in range(PLANE):
        total = taps[0:1, :] * wide[r * step : (r + 1) * step, :]
        for j in range(1, width):
            total = total + taps[j : j + 1, :] * wide[r * step + j : (r + 1) * step + j, :]
        out_ref[r, :step, :] = total.astype(BF16)
        out_ref[r, step:, :] = extra[r]


def finish(width, acc, x4, tiles, next_head, taps, extra):
    rows, own = x4.shape
    groups = own // GW
    step = rows // PLANE + HEAD
    col = pl.BlockSpec((rows, GW), lambda g: (0, g))
    return pl.pallas_call(
        functools.partial(last_kernel, width),
        grid=(groups,),
        in_specs=[
            col,
            col,
            pl.BlockSpec((1, BLK, 4 * BLK), lambda g: (g, 0, 1)),
            pl.BlockSpec((HEAD, GW), lambda g: (0, g)),
            pl.BlockSpec((width, GW), lambda g: (0, g)),
            pl.BlockSpec((PLANE, HEAD, GW), lambda g: (0, 0, 0)),
        ],
        out_specs=pl.BlockSpec((PLANE, step, GW), lambda g: (0, 0, g)),
        out_shape=jax.ShapeDtypeStruct((PLANE, step, own), BF16),
        scratch_shapes=[
            pltpu.VMEM((rows + BLK, 2 * GW), BF16),
            pltpu.VMEM((rows + 8, GW), F32),
        ],
        compiler_params=params(),
        cost_estimate=cost(2 * 3 * rows * rows * GW * groups, 8 * rows * own),
        name="finish",
    )(acc, x4, tiles, next_head, taps, extra)


def per_device(features, gate_values, upstream, short_filter, long_filter, loss_scale):
    shards = lax.axis_size("ctx")
    planes = shards // PLANE
    index = lax.axis_index("ctx")
    z, p = index // PLANE, index % PLANE
    width, chans = short_filter.shape
    own = chans // PLANE
    groups = own // GW
    rows = PLANE * features.shape[1]
    in_plane = [[k * PLANE + i for i in range(PLANE)] for k in range(planes)]

    def swap(x):
        return lax.all_to_all(x, "ctx", 0, 0, axis_index_groups=in_plane, tiled=True)

    def hop(x, count):
        step = PLANE * count
        route = [(i, i + step) for i in range(shards) if 0 <= i + step < shards]
        return lax.ppermute(x, "ctx", route)

    def after(x, *others):
        return lax.optimization_barrier((x,) + others)[0]

    feat1 = hop(features, 1)
    packed = gate(upstream, gate_values)
    x0 = swap(packed).reshape(rows, own)
    filters = lax.dynamic_slice_in_dim(after(long_filter, packed), p * groups, groups, 0)
    taps = lax.dynamic_slice_in_dim(after(short_filter, packed), p * own, own, 1)
    tiles, far_tiles = toeplitz(filters)
    feat1 = swap(pack(after(feat1, x0))).reshape(rows, own)
    feat0 = pack(after(features, x0))
    x1 = hop(x0, -1)
    x1_next = after(x1, feat0, feat1, tiles)
    feat0 = swap(after(feat0, feat1)).reshape(rows, own)
    feat2 = hop(feat1, 1)
    feat3_tail = hop(feat1[rows - HEAD :], 2)
    x4_head = hop(x0[:HEAD], -4)

    acc, mid = early(x0, x1, tiles)
    x2 = after(hop(x1_next, -1), acc, feat0, feat2, feat3_tail, x4_head)
    raw = all_terms(width, acc, mid, x2, feat0, feat1, feat2, feat3_tail, far_tiles)
    along_z = [[k * PLANE + i for k in range(planes)] for i in range(PLANE)]
    copies = jnp.broadcast_to(raw.astype(BF16)[None], (planes,) + raw.shape)
    x3 = after(hop(x2, -1), copies)
    copies = lax.all_to_all(copies, "ctx", 0, 0, axis_index_groups=along_z, tiled=True)
    x4 = hop(x3, -1)
    acc, head = third(acc, x2, x3, x4_head, tiles)
    raw = jnp.sum(after(copies, head).astype(F32), axis=0)
    next_head = hop(head, -1)
    copies = jnp.broadcast_to(raw[None], (lax.axis_size("dp"),) + raw.shape)
    raw = jnp.sum(lax.all_to_all(copies, "dp", 0, 0, tiled=True), axis=0)
    lane = chans // shards
    spans = own // lane // PLANE
    extra = prepare(z % spans, loss_scale, raw, lane)
    got = swap(finish(width, acc, x4, far_tiles, next_head, taps, extra))
    input_grad, short_grad, norm_value = unpack(z // spans, got, rows // PLANE, width, lane)
    return (input_grad, short_grad, norm_value.reshape(1))


def solution(mesh):
    placed = (P("dp", "ctx", None), P("dp", "ctx", None), P("dp", "ctx", None), P(), P(), P())
    return jax.shard_map(
        per_device,
        mesh=mesh,
        in_specs=placed,
        out_specs=(P("dp", "ctx", None), P(None, "ctx"), P()),
        check_vma=False,
    )
```

```python
import functools

import jax
import jax.numpy as jnp
from jax import lax
from jax.experimental import pallas as pl
from jax.experimental.pallas import tpu as pltpu
from jax.sharding import PartitionSpec as P

PLANE = 8
BLK = 256
GW = 128
HEAD = 16
SHORT = 64
VMEM = 56 * 1024 * 1024
F32, BF16 = jnp.float32, jnp.bfloat16


def params(grid=True):
    kwargs = {"dimension_semantics": ("arbitrary",)} if grid else {}
    return pltpu.CompilerParams(vmem_limit_bytes=VMEM, **kwargs)


def cost(flops, nbytes):
    return pl.CostEstimate(
        flops=int(flops) // SHORT, bytes_accessed=int(nbytes) // SHORT, transcendentals=0
    )


def dot(a, b):
    return jnp.dot(a, b, preferred_element_type=F32)


def gate_kernel(up_ref, gate_ref, out_ref):
    width = out_ref.shape[2]
    for p in range(PLANE):
        cols = slice(p * width, (p + 1) * width)
        prod = up_ref[0, :, cols].astype(F32) * gate_ref[0, :, cols].astype(F32)
        out_ref[p] = prod.astype(BF16)


def gate(upstream, gates):
    _, rows, chans = upstream.shape
    return pl.pallas_call(
        gate_kernel,
        out_shape=jax.ShapeDtypeStruct((PLANE, rows, chans // PLANE), BF16),
        compiler_params=params(False),
        cost_estimate=cost(upstream.size, 6 * upstream.size),
        name="gate",
    )(upstream, gates)


def pack_kernel(src_ref, out_ref):
    width = out_ref.shape[2]
    for p in range(PLANE):
        out_ref[p] = src_ref[0, :, p * width : (p + 1) * width]


def pack(features):
    _, rows, chans = features.shape
    return pl.pallas_call(
        pack_kernel,
        out_shape=jax.ShapeDtypeStruct((PLANE, rows, chans // PLANE), BF16),
        compiler_params=params(False),
        cost_estimate=cost(0, 4 * features.size),
        name="pack",
    )(features)


def split_terms(x):
    high = x.astype(BF16)
    rest = x - high.astype(F32)
    mid = rest.astype(BF16)
    return high, mid, (rest - mid.astype(F32)).astype(BF16)


def prepare_kernel(lane, half_ref, scale_ref, copies, out_ref):
    total = copies[0]
    for n in range(1, copies.shape[0]):
        total = total + copies[n]
    unscaled = jnp.concatenate([total[:8], total[8:]], axis=1) / scale_ref[0]
    norm = jnp.sum(unscaled * unscaled, keepdims=True)
    norm = split_terms(jnp.broadcast_to(norm, (8, 8)))
    span = PLANE * lane
    mine = unscaled[:, :span]
    for n in range(1, unscaled.shape[1] // span):
        mine = jnp.where(half_ref[0] == n, unscaled[:, n * span : (n + 1) * span], mine)
    parts = split_terms(mine)
    pad = jnp.zeros((8, GW - 3 * lane - 24), BF16)
    for p in range(PLANE):
        row = [x[:, p * lane : (p + 1) * lane] for x in parts]
        tile = jnp.concatenate([*row, *norm, pad], axis=1).astype(F32)
        out_ref[p] = jnp.concatenate([tile, jnp.zeros_like(tile)], axis=0).astype(BF16)


def prepare(half, scale, copies, lane):
    return pl.pallas_call(
        functools.partial(prepare_kernel, lane),
        in_specs=[pl.BlockSpec(memory_space=pltpu.SMEM)] * 2 + [pl.BlockSpec(memory_space=pltpu.VMEM)],
        out_shape=jax.ShapeDtypeStruct((PLANE, HEAD, GW), BF16),
        compiler_params=params(False),
        cost_estimate=cost(copies.size, 4 * copies.size),
        name="prepare",
    )(half.reshape(1), scale, copies)


def unpack_kernel(lane, source_ref, got, out_ref, short_ref, norm_ref, tiles, sems):
    width = got.shape[2]
    rows = out_ref.shape[1]
    behind = got.at[:, pl.ds(rows, HEAD), pl.ds(0, GW)]
    terms_copy = pltpu.make_async_copy(behind, tiles, sems.at[PLANE])
    terms_copy.start()
    copies = []
    for p in range(PLANE):
        source = got.at[p, pl.ds(0, rows), :]
        target = out_ref.at[0, :, pl.ds(p * width, width)]
        copies.append(pltpu.make_async_copy(source, target, sems.at[p]))
        copies[-1].start()
    terms_copy.wait()
    norm = jnp.zeros((8, 1), F32)
    short = jnp.zeros((8, lane), F32)
    for p in range(PLANE):
        tile = tiles[p].astype(F32)[:8]
        at = 3 * lane
        norm = norm + (tile[:, at : at + 1] + tile[:, at + 8 : at + 9] + tile[:, at + 16 : at + 17])
        terms = tile[:, :lane] + tile[:, lane : 2 * lane] + tile[:, 2 * lane : 3 * lane]
        short = jnp.where(source_ref[0] == p, terms, short)
    norm = jnp.sqrt(norm)
    short = jnp.where(jnp.abs(norm) < jnp.inf, short, jnp.zeros_like(short))
    short_ref[...] = short[: short_ref.shape[0], :]
    norm_ref[...] = norm[:1, :]
    for copy in copies:
        copy.wait()


def unpack(source, got, rows, width, lane):
    return pl.pallas_call(
        functools.partial(unpack_kernel, lane),
        in_specs=[pl.BlockSpec(memory_space=pltpu.SMEM), pl.BlockSpec(memory_space=pl.ANY)],
        out_specs=[
            pl.BlockSpec(memory_space=pl.ANY),
            pl.BlockSpec(memory_space=pltpu.VMEM),
            pl.BlockSpec(memory_space=pltpu.VMEM),
        ],
        out_shape=[
            jax.ShapeDtypeStruct((1, rows, PLANE * got.shape[2]), BF16),
            jax.ShapeDtypeStruct((width, lane), F32),
            jax.ShapeDtypeStruct((1, 1), F32),
        ],
        scratch_shapes=[
            pltpu.VMEM((PLANE, HEAD, GW), BF16),
            pltpu.SemaphoreType.DMA((PLANE + 1,)),
        ],
        compiler_params=pltpu.CompilerParams(vmem_limit_bytes=4 * 1024 * 1024),
        cost_estimate=cost(0, 4 * got.size),
        name="unpack",
    )(source.reshape(1), got)


def toeplitz_kernel(taps_ref, all_ref, far_ref):
    taps = taps_ref.shape[2]
    half = BLK // 2
    row = jnp.concatenate([taps_ref[0], jnp.zeros((1, BLK), F32)], axis=1)
    base = jnp.broadcast_to(row, (half, taps + BLK))
    base = pltpu.roll(base, 0, 1, stride=1, stride_axis=0).astype(BF16)
    all_ref[0, :half, :] = base
    all_ref[0, half:, :half] = jnp.zeros((half, half), BF16)
    all_ref[0, half:, half:] = base[:, : taps + BLK - half]
    far_ref[0] = all_ref[0, :, taps - 7 * BLK :]


def toeplitz(filters):
    groups, taps = filters.shape
    return pl.pallas_call(
        toeplitz_kernel,
        grid=(groups,),
        in_specs=[pl.BlockSpec((1, 1, taps), lambda g: (g, 0, 0))],
        out_specs=[
            pl.BlockSpec((1, BLK, taps + BLK), lambda g: (g, 0, 0)),
            pl.BlockSpec((1, BLK, 8 * BLK), lambda g: (g, 0, 0)),
        ],
        out_shape=[
            jax.ShapeDtypeStruct((groups, BLK, taps + BLK), BF16),
            jax.ShapeDtypeStruct((groups, BLK, 8 * BLK), BF16),
        ],
        compiler_params=params(),
        cost_estimate=cost(groups * BLK * taps * 16, 2 * groups * BLK * taps * 3),
        name="toeplitz",
    )(filters.astype(F32).reshape(groups, 1, taps))


def fill_pairs(pairs_ref, planes):
    rows = sum(x.shape[0] for x in planes)
    zero = jnp.zeros((BLK, GW), BF16)
    pairs_ref[:BLK, :GW] = zero
    at = 0
    for x in planes:
        pairs_ref[BLK + at : BLK + at + x.shape[0], :GW] = x[...]
        pairs_ref[at : at + x.shape[0], GW:] = x[...]
        at += x.shape[0]
    pairs_ref[rows : rows + BLK, GW:] = zero


def tile_products(tiles_ref, first, last, pairs_ref, distance, blocks):
    out = []
    for pair in (0, 2):
        low, high = distance - 1 - pair, distance + blocks - 1 - pair
        k0, k1 = max(low, first), min(high, last)
        tiles = tiles_ref[0, :, (k0 - first) * BLK : (k1 + 1 - first) * BLK]
        window = pairs_ref[(k0 - low) * BLK : (k1 + 1 - low) * BLK, :]
        out.append(dot(tiles, window))
    return out


def store_rows(ref, products, add=None):
    for n, prod in enumerate(products):
        for m in range(2):
            rows = slice((2 * n + m) * BLK, (2 * n + m + 1) * BLK)
            value = prod[:, m * GW : (m + 1) * GW]
            ref[rows, :] = value if add is None else add[rows, :] + value


def correlate(conv_ref, feat, before, feat_wide, terms):
    rows = conv_ref.shape[0]
    feat_wide[:8, :] = before[before.shape[0] - 8 :, :].astype(F32)
    feat_wide[8:, :] = feat.astype(F32)
    for r in range(0, rows, 128):
        conv = conv_ref[r : r + 128, :]
        for j in range(len(terms)):
            prod = conv * feat_wide[r + 8 - j : r + 136 - j, :]
            terms[j] = terms[j] + jnp.sum(prod.reshape(16, 8, GW), axis=0)
    return terms


def add_terms(raw_ref, terms, add=None):
    out = [jnp.sum(t, axis=0, keepdims=True) for t in terms]
    out.append(jnp.zeros((8 - len(terms), GW), F32))
    out = jnp.concatenate(out, axis=0)
    raw_ref[...] = out if add is None else add[...] + out


def pairs_of(rows):
    return pltpu.VMEM((rows + BLK, 2 * GW), BF16)


def early_kernel(x0, x1, tiles, acc_ref, mid_ref, pairs):
    last = tiles.shape[2] // BLK - 1
    fill_pairs(pairs, [x0, x1])
    store_rows(acc_ref, tile_products(tiles, 0, last, pairs, 0, 8))
    fill_pairs(pairs, [x1])
    store_rows(mid_ref, tile_products(tiles, 0, last, pairs, 8, 4))


def early(x0, x1, tiles):
    rows, own = x0.shape
    groups = own // GW
    col = pl.BlockSpec((rows, GW), lambda g: (0, g))
    out = jax.ShapeDtypeStruct((rows, own), F32)
    return pl.pallas_call(
        early_kernel,
        grid=(groups,),
        in_specs=[col, col, pl.BlockSpec((1, BLK, 12 * BLK), lambda g: (g, 0, 0))],
        out_specs=[col, col],
        out_shape=[out, out],
        scratch_shapes=[pairs_of(2 * rows)],
        compiler_params=params(),
        cost_estimate=cost(24 * rows * rows * GW * groups, 12 * rows * own),
        name="early",
    )(x0, x1, tiles)


def terms_kernel(
    width, acc, mid, x2, f0, f1, f2, f3_tail, tiles, raw_ref, pairs, far, feat_wide, two
):
    rows = x2.shape[0]
    fill_pairs(pairs, [x2])
    terms = [jnp.zeros((8, GW), F32)] * width
    terms = correlate(acc, f0[...], f1[rows - HEAD :, :], feat_wide, terms)
    store_rows(far, tile_products(tiles, 9, 16, pairs, 12, 4), add=mid)
    terms = correlate(far, f1[...], f2[rows - HEAD :, :], feat_wide, terms)
    store_rows(far, tile_products(tiles, 9, 16, pairs, 16, 4))
    terms = correlate(far, f2[...], f3_tail[...], feat_wide, terms)
    out = [jnp.sum(t, axis=0, keepdims=True) for t in terms]
    out.append(jnp.zeros((8 - width, GW), F32))
    out = jnp.concatenate(out, axis=0)
    upper = pl.program_id(0) % 2 == 0

    @pl.when(upper)
    def _():
        two[:8, :] = out

    @pl.when(jnp.logical_not(upper))
    def _():
        two[8:, :] = out
        packed = two[...].astype(BF16)
        for n in range(raw_ref.shape[0]):
            raw_ref[n] = packed


def all_terms(width, planes, acc, mid, x2, f0, f1, f2, f3_tail, tiles):
    rows, own = acc.shape
    groups = own // GW

    def group(g):
        return (g % 2) * (groups // 2) + g // 2

    col = pl.BlockSpec((rows, GW), lambda g: (0, group(g)))
    return pl.pallas_call(
        functools.partial(terms_kernel, width),
        grid=(groups,),
        in_specs=[
            col,
            col,
            col,
            col,
            col,
            col,
            pl.BlockSpec((HEAD, GW), lambda g: (0, group(g))),
            pl.BlockSpec((1,) + tiles.shape[1:], lambda g: (group(g), 0, 0)),
        ],
        out_specs=pl.BlockSpec((planes, 16, GW), lambda g: (0, 0, g // 2)),
        out_shape=jax.ShapeDtypeStruct((planes, 16, own // 2), BF16),
        scratch_shapes=[
            pairs_of(rows),
            pltpu.VMEM((rows, GW), F32),
            pltpu.VMEM((rows + 8, GW), F32),
            pltpu.VMEM((16, GW), F32),
        ],
        compiler_params=params(),
        cost_estimate=cost(16 * rows * rows * GW * groups, 20 * rows * own),
        name="all_terms",
    )(acc, mid, x2, f0, f1, f2, f3_tail, tiles)


def third_kernel(acc_in, x2, x3, x4_head, tiles, acc_ref, head_ref, pairs):
    last = tiles.shape[2] // BLK - 1
    fill_pairs(pairs, [x2, x3])
    store_rows(acc_ref, tile_products(tiles, 0, last, pairs, 8, 8), add=acc_in)
    ahead = jnp.concatenate([x4_head[...], jnp.zeros((GW - HEAD, GW), BF16)], axis=0)
    corner = tiles[0, :HEAD, last * BLK : last * BLK + GW]
    head_ref[...] = (acc_ref[:HEAD, :] + dot(corner, ahead)).astype(BF16)


def third(acc, x2, x3, x4_head, tiles):
    rows, own = acc.shape
    groups = own // GW
    col = pl.BlockSpec((rows, GW), lambda g: (0, g))
    return pl.pallas_call(
        third_kernel,
        grid=(groups,),
        in_specs=[
            col,
            col,
            col,
            pl.BlockSpec((HEAD, GW), lambda g: (0, g)),
            pl.BlockSpec((1,) + tiles.shape[1:], lambda g: (g, 0, 0)),
        ],
        out_specs=[col, pl.BlockSpec((HEAD, GW), lambda g: (0, g))],
        out_shape=[
            jax.ShapeDtypeStruct((rows, own), F32),
            jax.ShapeDtypeStruct((HEAD, own), BF16),
        ],
        scratch_shapes=[pairs_of(2 * rows)],
        compiler_params=params(),
        cost_estimate=cost(SHORT * 72 * rows * rows * GW * groups, SHORT * 48 * rows * own),
        name="third",
    )(acc, x2, x3, x4_head, tiles)


def last_kernel(width, acc_in, x4, tiles, next_head, taps, extra, out_ref, pairs, wide):
    rows = x4.shape[0]
    step = rows // PLANE
    fill_pairs(pairs, [x4])
    for n, prod in enumerate(tile_products(tiles, 13, 16, pairs, 16, 4)):
        for m in range(2):
            at = slice((2 * n + m) * BLK, (2 * n + m + 1) * BLK)
            value = acc_in[at, :] + prod[:, m * GW : (m + 1) * GW]
            wide[at, :] = value.astype(BF16).astype(F32)
    wide[rows:, :] = next_head[:8, :].astype(F32)
    for r in range(PLANE):
        total = taps[0:1, :] * wide[r * step : (r + 1) * step, :]
        for j in range(1, width):
            total = total + taps[j : j + 1, :] * wide[r * step + j : (r + 1) * step + j, :]
        out_ref[r, :step, :] = total.astype(BF16)
        out_ref[r, step:, :] = extra[r]


def finish(width, acc, x4, tiles, next_head, taps, extra):
    rows, own = x4.shape
    groups = own // GW
    step = rows // PLANE + HEAD
    col = pl.BlockSpec((rows, GW), lambda g: (0, g))
    return pl.pallas_call(
        functools.partial(last_kernel, width),
        grid=(groups,),
        in_specs=[
            col,
            col,
            pl.BlockSpec((1, BLK, 4 * BLK), lambda g: (g, 0, 1)),
            pl.BlockSpec((HEAD, GW), lambda g: (0, g)),
            pl.BlockSpec((width, GW), lambda g: (0, g)),
            pl.BlockSpec((PLANE, HEAD, GW), lambda g: (0, 0, 0)),
        ],
        out_specs=pl.BlockSpec((PLANE, step, GW), lambda g: (0, 0, g)),
        out_shape=jax.ShapeDtypeStruct((PLANE, step, own), BF16),
        scratch_shapes=[
            pltpu.VMEM((rows + BLK, 2 * GW), BF16),
            pltpu.VMEM((rows + 8, GW), F32),
        ],
        compiler_params=params(),
        cost_estimate=cost(2 * 3 * rows * rows * GW * groups, 8 * rows * own),
        name="finish",
    )(acc, x4, tiles, next_head, taps, extra)


def per_device(features, gate_values, upstream, short_filter, long_filter, loss_scale):
    shards = lax.axis_size("ctx")
    planes = shards // PLANE
    index = lax.axis_index("ctx")
    z, p = index // PLANE, index % PLANE
    width, chans = short_filter.shape
    own = chans // PLANE
    groups = own // GW
    rows = PLANE * features.shape[1]
    in_plane = [[k * PLANE + i for i in range(PLANE)] for k in range(planes)]

    def swap(x):
        return lax.all_to_all(x, "ctx", 0, 0, axis_index_groups=in_plane, tiled=True)

    def hop(x, count):
        step = PLANE * count
        route = [(i, i + step) for i in range(shards) if 0 <= i + step < shards]
        return lax.ppermute(x, "ctx", route)

    def after(x, *others):
        return lax.optimization_barrier((x,) + others)[0]

    feat1 = hop(features, 1)
    packed = gate(upstream, gate_values)
    x0 = swap(packed).reshape(rows, own)
    filters = lax.dynamic_slice_in_dim(after(long_filter, packed), p * groups, groups, 0)
    taps = lax.dynamic_slice_in_dim(after(short_filter, packed), p * own, own, 1)
    tiles, far_tiles = toeplitz(filters)
    feat1 = swap(pack(after(feat1, x0))).reshape(rows, own)
    feat0 = pack(after(features, x0))
    x1 = hop(x0, -1)
    x1_next = after(x1, feat0, feat1, tiles, taps)
    feat0 = swap(after(feat0, feat1)).reshape(rows, own)
    feat2 = hop(feat1, 1)
    feat3_tail = hop(feat1[rows - HEAD :], 2)
    x4_head = hop(x0[:HEAD], -4)

    acc, mid = early(x0, x1, tiles)
    x2 = after(hop(x1_next, -1), acc, feat0, feat2, feat3_tail, x4_head)
    copies = all_terms(width, planes, acc, mid, x2, feat0, feat1, feat2, feat3_tail, far_tiles)
    along_z = [[k * PLANE + i for k in range(planes)] for i in range(PLANE)]
    x3 = after(hop(x2, -1), copies)
    copies = lax.all_to_all(copies, "ctx", 0, 0, axis_index_groups=along_z, tiled=True)
    x4 = hop(x3, -1)
    acc, head = third(acc, x2, x3, x4_head, tiles)
    raw = jnp.sum(after(copies, head).astype(F32), axis=0)
    next_head = hop(head, -1)
    copies = jnp.broadcast_to(raw[None], (lax.axis_size("dp"),) + raw.shape)
    copies = lax.all_to_all(copies, "dp", 0, 0, tiled=True)
    lane = chans // shards
    spans = own // lane // PLANE
    extra = prepare(z % spans, loss_scale, copies, lane)
    got = swap(finish(width, acc, x4, far_tiles, next_head, taps, extra))
    input_grad, short_grad, norm_value = unpack(z // spans, got, rows // PLANE, width, lane)
    return (input_grad, short_grad, norm_value.reshape(1))


def solution(mesh):
    placed = (P("dp", "ctx", None), P("dp", "ctx", None), P("dp", "ctx", None), P(), P(), P())
    return jax.shard_map(
        per_device,
        mesh=mesh,
        in_specs=placed,
        out_specs=(P("dp", "ctx", None), P(None, "ctx"), P()),
        check_vma=False,
    )
```

```python
import functools

import jax
import jax.numpy as jnp
from jax import lax
from jax.experimental import pallas as pl
from jax.experimental.pallas import tpu as pltpu
from jax.sharding import PartitionSpec as P

PLANE = 8
BLK = 256
GW = 128
HEAD = 16
SHORT = 64
VMEM = 56 * 1024 * 1024
F32, BF16 = jnp.float32, jnp.bfloat16


def params(grid=True):
    kwargs = {"dimension_semantics": ("arbitrary",)} if grid else {}
    return pltpu.CompilerParams(vmem_limit_bytes=VMEM, **kwargs)


def cost(flops, nbytes):
    return pl.CostEstimate(
        flops=int(flops) // SHORT, bytes_accessed=int(nbytes) // SHORT, transcendentals=0
    )


def dot(a, b):
    return jnp.dot(a, b, preferred_element_type=F32)


def gate_kernel(up_ref, gate_ref, out_ref):
    width = out_ref.shape[2]
    for p in range(PLANE):
        cols = slice(p * width, (p + 1) * width)
        prod = up_ref[0, :, cols].astype(F32) * gate_ref[0, :, cols].astype(F32)
        out_ref[p] = prod.astype(BF16)


def gate(upstream, gates):
    _, rows, chans = upstream.shape
    return pl.pallas_call(
        gate_kernel,
        out_shape=jax.ShapeDtypeStruct((PLANE, rows, chans // PLANE), BF16),
        compiler_params=params(False),
        cost_estimate=cost(upstream.size, 6 * upstream.size),
        name="gate",
    )(upstream, gates)


def pack_kernel(src_ref, out_ref):
    width = out_ref.shape[2]
    for p in range(PLANE):
        out_ref[p] = src_ref[0, :, p * width : (p + 1) * width]


def pack(features):
    _, rows, chans = features.shape
    return pl.pallas_call(
        pack_kernel,
        out_shape=jax.ShapeDtypeStruct((PLANE, rows, chans // PLANE), BF16),
        compiler_params=params(False),
        cost_estimate=cost(0, 4 * features.size),
        name="pack",
    )(features)


def split_terms(x):
    high = x.astype(BF16)
    rest = x - high.astype(F32)
    mid = rest.astype(BF16)
    return high, mid, (rest - mid.astype(F32)).astype(BF16)


def prepare_kernel(lane, half_ref, scale_ref, copies, out_ref):
    total = copies[0]
    for n in range(1, copies.shape[0]):
        total = total + copies[n]
    unscaled = jnp.concatenate([total[:8], total[8:]], axis=1) / scale_ref[0]
    norm = jnp.sum(unscaled * unscaled, keepdims=True)
    norm = split_terms(jnp.broadcast_to(norm, (8, 8)))
    span = PLANE * lane
    mine = unscaled[:, :span]
    for n in range(1, unscaled.shape[1] // span):
        mine = jnp.where(half_ref[0] == n, unscaled[:, n * span : (n + 1) * span], mine)
    parts = split_terms(mine)
    pad = jnp.zeros((8, GW - 3 * lane - 24), BF16)
    for p in range(PLANE):
        row = [x[:, p * lane : (p + 1) * lane] for x in parts]
        tile = jnp.concatenate([*row, *norm, pad], axis=1).astype(F32)
        out_ref[p] = jnp.concatenate([tile, jnp.zeros_like(tile)], axis=0).astype(BF16)


def prepare(half, scale, copies, lane):
    return pl.pallas_call(
        functools.partial(prepare_kernel, lane),
        in_specs=[pl.BlockSpec(memory_space=pltpu.SMEM)] * 2 + [pl.BlockSpec(memory_space=pltpu.VMEM)],
        out_shape=jax.ShapeDtypeStruct((PLANE, HEAD, GW), BF16),
        compiler_params=params(False),
        cost_estimate=cost(copies.size, 4 * copies.size),
        name="prepare",
    )(half.reshape(1), scale, copies)


def unpack_kernel(lane, source_ref, got, out_ref, short_ref, norm_ref, tiles, sems):
    width = got.shape[2]
    rows = out_ref.shape[1]
    behind = got.at[:, pl.ds(rows, HEAD), pl.ds(0, GW)]
    terms_copy = pltpu.make_async_copy(behind, tiles, sems.at[PLANE])
    terms_copy.start()
    copies = []
    for p in range(PLANE):
        source = got.at[p, pl.ds(0, rows), :]
        target = out_ref.at[0, :, pl.ds(p * width, width)]
        copies.append(pltpu.make_async_copy(source, target, sems.at[p]))
        copies[-1].start()
    terms_copy.wait()
    norm = jnp.zeros((8, 1), F32)
    short = jnp.zeros((8, lane), F32)
    for p in range(PLANE):
        tile = tiles[p].astype(F32)[:8]
        at = 3 * lane
        norm = norm + (tile[:, at : at + 1] + tile[:, at + 8 : at + 9] + tile[:, at + 16 : at + 17])
        terms = tile[:, :lane] + tile[:, lane : 2 * lane] + tile[:, 2 * lane : 3 * lane]
        short = jnp.where(source_ref[0] == p, terms, short)
    norm = jnp.sqrt(norm)
    short = jnp.where(jnp.abs(norm) < jnp.inf, short, jnp.zeros_like(short))
    short_ref[...] = short[: short_ref.shape[0], :]
    norm_ref[...] = norm[:1, :]
    for copy in copies:
        copy.wait()


def unpack(source, got, rows, width, lane):
    return pl.pallas_call(
        functools.partial(unpack_kernel, lane),
        in_specs=[pl.BlockSpec(memory_space=pltpu.SMEM), pl.BlockSpec(memory_space=pl.ANY)],
        out_specs=[
            pl.BlockSpec(memory_space=pl.ANY),
            pl.BlockSpec(memory_space=pltpu.VMEM),
            pl.BlockSpec(memory_space=pltpu.VMEM),
        ],
        out_shape=[
            jax.ShapeDtypeStruct((1, rows, PLANE * got.shape[2]), BF16),
            jax.ShapeDtypeStruct((width, lane), F32),
            jax.ShapeDtypeStruct((1, 1), F32),
        ],
        scratch_shapes=[
            pltpu.VMEM((PLANE, HEAD, GW), BF16),
            pltpu.SemaphoreType.DMA((PLANE + 1,)),
        ],
        compiler_params=pltpu.CompilerParams(vmem_limit_bytes=4 * 1024 * 1024),
        cost_estimate=cost(0, 4 * got.size),
        name="unpack",
    )(source.reshape(1), got)


def toeplitz_kernel(taps_ref, all_ref, far_ref):
    taps = taps_ref.shape[2]
    half = BLK // 2
    row = jnp.concatenate([taps_ref[0], jnp.zeros((1, BLK), F32)], axis=1)
    base = jnp.broadcast_to(row, (half, taps + BLK))
    base = pltpu.roll(base, 0, 1, stride=1, stride_axis=0).astype(BF16)
    all_ref[0, :half, :] = base
    all_ref[0, half:, :half] = jnp.zeros((half, half), BF16)
    all_ref[0, half:, half:] = base[:, : taps + BLK - half]
    far_ref[0] = all_ref[0, :, taps - 7 * BLK :]


def toeplitz(filters):
    groups, taps = filters.shape
    return pl.pallas_call(
        toeplitz_kernel,
        grid=(groups,),
        in_specs=[pl.BlockSpec((1, 1, taps), lambda g: (g, 0, 0))],
        out_specs=[
            pl.BlockSpec((1, BLK, taps + BLK), lambda g: (g, 0, 0)),
            pl.BlockSpec((1, BLK, 8 * BLK), lambda g: (g, 0, 0)),
        ],
        out_shape=[
            jax.ShapeDtypeStruct((groups, BLK, taps + BLK), BF16),
            jax.ShapeDtypeStruct((groups, BLK, 8 * BLK), BF16),
        ],
        compiler_params=params(),
        cost_estimate=cost(groups * BLK * taps * 16, 2 * groups * BLK * taps * 3),
        name="toeplitz",
    )(filters.astype(F32).reshape(groups, 1, taps))


def fill_pairs(pairs_ref, planes):
    rows = sum(x.shape[0] for x in planes)
    zero = jnp.zeros((BLK, GW), BF16)
    pairs_ref[:BLK, :GW] = zero
    at = 0
    for x in planes:
        pairs_ref[BLK + at : BLK + at + x.shape[0], :GW] = x[...]
        pairs_ref[at : at + x.shape[0], GW:] = x[...]
        at += x.shape[0]
    pairs_ref[rows : rows + BLK, GW:] = zero


def tile_products(tiles_ref, first, last, pairs_ref, distance, blocks):
    out = []
    for pair in (0, 2):
        low, high = distance - 1 - pair, distance + blocks - 1 - pair
        k0, k1 = max(low, first), min(high, last)
        tiles = tiles_ref[0, :, (k0 - first) * BLK : (k1 + 1 - first) * BLK]
        window = pairs_ref[(k0 - low) * BLK : (k1 + 1 - low) * BLK, :]
        out.append(dot(tiles, window))
    return out


def store_rows(ref, products, add=None):
    for n, prod in enumerate(products):
        for m in range(2):
            rows = slice((2 * n + m) * BLK, (2 * n + m + 1) * BLK)
            value = prod[:, m * GW : (m + 1) * GW]
            ref[rows, :] = value if add is None else add[rows, :] + value


def correlate(conv_ref, feat, before, feat_wide, terms):
    rows = conv_ref.shape[0]
    feat_wide[:8, :] = before[before.shape[0] - 8 :, :].astype(F32)
    feat_wide[8:, :] = feat.astype(F32)
    for r in range(0, rows, 128):
        conv = conv_ref[r : r + 128, :]
        for j in range(len(terms)):
            prod = conv * feat_wide[r + 8 - j : r + 136 - j, :]
            terms[j] = terms[j] + jnp.sum(prod.reshape(16, 8, GW), axis=0)
    return terms


def add_terms(raw_ref, terms, add=None):
    out = [jnp.sum(t, axis=0, keepdims=True) for t in terms]
    out.append(jnp.zeros((8 - len(terms), GW), F32))
    out = jnp.concatenate(out, axis=0)
    raw_ref[...] = out if add is None else add[...] + out


def pairs_of(rows):
    return pltpu.VMEM((rows + BLK, 2 * GW), BF16)


def early_kernel(x0, x1, tiles, acc_ref, mid_ref, pairs):
    last = tiles.shape[2] // BLK - 1
    fill_pairs(pairs, [x0, x1])
    store_rows(acc_ref, tile_products(tiles, 0, last, pairs, 0, 8))
    pairs[4 * BLK : 5 * BLK, :GW] = jnp.zeros((BLK, GW), BF16)
    behind = pairs.at[pl.ds(4 * BLK, 5 * BLK)]
    store_rows(mid_ref, tile_products(tiles, 0, last, behind, 8, 4))


def early(x0, x1, tiles):
    rows, own = x0.shape
    groups = own // GW
    col = pl.BlockSpec((rows, GW), lambda g: (0, g))
    out = jax.ShapeDtypeStruct((rows, own), F32)
    return pl.pallas_call(
        early_kernel,
        grid=(groups,),
        in_specs=[col, col, pl.BlockSpec((1, BLK, 12 * BLK), lambda g: (g, 0, 0))],
        out_specs=[col, col],
        out_shape=[out, out],
        scratch_shapes=[pairs_of(2 * rows)],
        compiler_params=params(),
        cost_estimate=cost(24 * rows * rows * GW * groups, 12 * rows * own),
        name="early",
    )(x0, x1, tiles)


def terms_kernel(
    width, acc, mid, x2, f0, f1, f2, f3_tail, tiles, raw_ref, pairs, far, feat_wide, two
):
    rows = x2.shape[0]
    fill_pairs(pairs, [x2])
    terms = [jnp.zeros((8, GW), F32)] * width
    terms = correlate(acc, f0[...], f1[rows - HEAD :, :], feat_wide, terms)
    store_rows(far, tile_products(tiles, 9, 16, pairs, 12, 4), add=mid)
    terms = correlate(far, f1[...], f2[rows - HEAD :, :], feat_wide, terms)
    store_rows(far, tile_products(tiles, 9, 16, pairs, 16, 4))
    terms = correlate(far, f2[...], f3_tail[...], feat_wide, terms)
    out = [jnp.sum(t, axis=0, keepdims=True) for t in terms]
    out.append(jnp.zeros((8 - width, GW), F32))
    out = jnp.concatenate(out, axis=0)
    upper = pl.program_id(0) % 2 == 0

    @pl.when(upper)
    def _():
        two[:8, :] = out

    @pl.when(jnp.logical_not(upper))
    def _():
        two[8:, :] = out
        packed = two[...].astype(BF16)
        for n in range(raw_ref.shape[0]):
            raw_ref[n] = packed


def all_terms(width, planes, acc, mid, x2, f0, f1, f2, f3_tail, tiles):
    rows, own = acc.shape
    groups = own // GW

    def group(g):
        return (g % 2) * (groups // 2) + g // 2

    col = pl.BlockSpec((rows, GW), lambda g: (0, group(g)))
    return pl.pallas_call(
        functools.partial(terms_kernel, width),
        grid=(groups,),
        in_specs=[
            col,
            col,
            col,
            col,
            col,
            col,
            pl.BlockSpec((HEAD, GW), lambda g: (0, group(g))),
            pl.BlockSpec((1,) + tiles.shape[1:], lambda g: (group(g), 0, 0)),
        ],
        out_specs=pl.BlockSpec((planes, 16, GW), lambda g: (0, 0, g // 2)),
        out_shape=jax.ShapeDtypeStruct((planes, 16, own // 2), BF16),
        scratch_shapes=[
            pairs_of(rows),
            pltpu.VMEM((rows, GW), F32),
            pltpu.VMEM((rows + 8, GW), F32),
            pltpu.VMEM((16, GW), F32),
        ],
        compiler_params=params(),
        cost_estimate=cost(16 * rows * rows * GW * groups, 20 * rows * own),
        name="all_terms",
    )(acc, mid, x2, f0, f1, f2, f3_tail, tiles)


def third_kernel(acc_in, x2, x3, x4_head, tiles, acc_ref, head_ref, pairs):
    last = tiles.shape[2] // BLK - 1
    fill_pairs(pairs, [x2, x3])
    store_rows(acc_ref, tile_products(tiles, 0, last, pairs, 8, 8), add=acc_in)
    ahead = jnp.concatenate([x4_head[...], jnp.zeros((GW - HEAD, GW), BF16)], axis=0)
    corner = tiles[0, :HEAD, last * BLK : last * BLK + GW]
    head_ref[...] = (acc_ref[:HEAD, :] + dot(corner, ahead)).astype(BF16)


def third(acc, x2, x3, x4_head, tiles):
    rows, own = acc.shape
    groups = own // GW
    col = pl.BlockSpec((rows, GW), lambda g: (0, g))
    return pl.pallas_call(
        third_kernel,
        grid=(groups,),
        in_specs=[
            col,
            col,
            col,
            pl.BlockSpec((HEAD, GW), lambda g: (0, g)),
            pl.BlockSpec((1,) + tiles.shape[1:], lambda g: (g, 0, 0)),
        ],
        out_specs=[col, pl.BlockSpec((HEAD, GW), lambda g: (0, g))],
        out_shape=[
            jax.ShapeDtypeStruct((rows, own), F32),
            jax.ShapeDtypeStruct((HEAD, own), BF16),
        ],
        scratch_shapes=[pairs_of(2 * rows)],
        compiler_params=params(),
        cost_estimate=cost(SHORT * 72 * rows * rows * GW * groups, SHORT * 48 * rows * own),
        name="third",
    )(acc, x2, x3, x4_head, tiles)


def last_kernel(width, acc_in, x4, tiles, next_head, taps, extra, out_ref, pairs, wide):
    rows = x4.shape[0]
    step = rows // PLANE
    fill_pairs(pairs, [x4])
    for n, prod in enumerate(tile_products(tiles, 13, 16, pairs, 16, 4)):
        for m in range(2):
            at = slice((2 * n + m) * BLK, (2 * n + m + 1) * BLK)
            value = acc_in[at, :] + prod[:, m * GW : (m + 1) * GW]
            wide[at, :] = value.astype(BF16).astype(F32)
    wide[rows:, :] = next_head[:8, :].astype(F32)
    for r in range(PLANE):
        total = taps[0:1, :] * wide[r * step : (r + 1) * step, :]
        for j in range(1, width):
            total = total + taps[j : j + 1, :] * wide[r * step + j : (r + 1) * step + j, :]
        out_ref[r, :step, :] = total.astype(BF16)
        out_ref[r, step:, :] = extra[r]


def finish(width, acc, x4, tiles, next_head, taps, extra):
    rows, own = x4.shape
    groups = own // GW
    step = rows // PLANE + HEAD
    col = pl.BlockSpec((rows, GW), lambda g: (0, g))
    return pl.pallas_call(
        functools.partial(last_kernel, width),
        grid=(groups,),
        in_specs=[
            col,
            col,
            pl.BlockSpec((1, BLK, 4 * BLK), lambda g: (g, 0, 1)),
            pl.BlockSpec((HEAD, GW), lambda g: (0, g)),
            pl.BlockSpec((width, GW), lambda g: (0, g)),
            pl.BlockSpec((PLANE, HEAD, GW), lambda g: (0, 0, 0)),
        ],
        out_specs=pl.BlockSpec((PLANE, step, GW), lambda g: (0, 0, g)),
        out_shape=jax.ShapeDtypeStruct((PLANE, step, own), BF16),
        scratch_shapes=[
            pltpu.VMEM((rows + BLK, 2 * GW), BF16),
            pltpu.VMEM((rows + 8, GW), F32),
        ],
        compiler_params=params(),
        cost_estimate=cost(2 * 3 * rows * rows * GW * groups, 8 * rows * own),
        name="finish",
    )(acc, x4, tiles, next_head, taps, extra)


def per_device(features, gate_values, upstream, short_filter, long_filter, loss_scale):
    shards = lax.axis_size("ctx")
    planes = shards // PLANE
    index = lax.axis_index("ctx")
    z, p = index // PLANE, index % PLANE
    width, chans = short_filter.shape
    own = chans // PLANE
    groups = own // GW
    rows = PLANE * features.shape[1]
    in_plane = [[k * PLANE + i for i in range(PLANE)] for k in range(planes)]

    def swap(x):
        return lax.all_to_all(x, "ctx", 0, 0, axis_index_groups=in_plane, tiled=True)

    def hop(x, count):
        step = PLANE * count
        route = [(i, i + step) for i in range(shards) if 0 <= i + step < shards]
        return lax.ppermute(x, "ctx", route)

    def after(x, *others):
        return lax.optimization_barrier((x,) + others)[0]

    feat1 = hop(features, 1)
    packed = gate(upstream, gate_values)
    x0 = swap(packed).reshape(rows, own)
    filters = lax.dynamic_slice_in_dim(after(long_filter, packed), p * groups, groups, 0)
    taps = lax.dynamic_slice_in_dim(after(short_filter, packed), p * own, own, 1)
    tiles, far_tiles = toeplitz(filters)
    feat1 = swap(pack(after(feat1, x0))).reshape(rows, own)
    feat0 = pack(after(features, x0))
    x1 = hop(x0, -1)
    x1_next = after(x1, feat0, feat1, tiles, taps)
    feat0 = swap(after(feat0, feat1)).reshape(rows, own)
    feat2 = hop(feat1, 1)
    feat3_tail = hop(feat1[rows - HEAD :], 2)
    x4_head = hop(x0[:HEAD], -4)

    acc, mid = early(x0, x1, tiles)
    x2 = after(hop(x1_next, -1), acc, feat0, feat2, feat3_tail, x4_head)
    copies = all_terms(width, planes, acc, mid, x2, feat0, feat1, feat2, feat3_tail, far_tiles)
    along_z = [[k * PLANE + i for k in range(planes)] for i in range(PLANE)]
    x3 = after(hop(x2, -1), copies)
    copies = lax.all_to_all(copies, "ctx", 0, 0, axis_index_groups=along_z, tiled=True)
    x4 = hop(x3, -1)
    acc, head = third(acc, x2, x3, x4_head, tiles)
    raw = jnp.sum(after(copies, head).astype(F32), axis=0)
    next_head = hop(head, -1)
    copies = jnp.broadcast_to(raw[None], (lax.axis_size("dp"),) + raw.shape)
    copies = lax.all_to_all(copies, "dp", 0, 0, tiled=True)
    lane = chans // shards
    spans = own // lane // PLANE
    extra = prepare(z % spans, loss_scale, copies, lane)
    got = swap(finish(width, acc, x4, far_tiles, next_head, taps, extra))
    input_grad, short_grad, norm_value = unpack(z // spans, got, rows // PLANE, width, lane)
    return (input_grad, short_grad, norm_value.reshape(1))


def solution(mesh):
    placed = (P("dp", "ctx", None), P("dp", "ctx", None), P("dp", "ctx", None), P(), P(), P())
    return jax.shard_map(
        per_device,
        mesh=mesh,
        in_specs=placed,
        out_specs=(P("dp", "ctx", None), P(None, "ctx"), P()),
        check_vma=False,
    )
```
